128 devices in a mesh: chan: 16 (over y, z_lo, core), ctx: 8 (over x, z_hi).
Axes of the slice: x: 4, y: 4, z: 4 (z_hi: 2, z_lo: 2; z = z_hi * 2 + z_lo), core: 2. Of those that a mesh axis runs over, the one named last changes fastest.
Arguments:
- grad_out: bfloat16 [16384, 4096], P('ctx', 'chan'), may hold values from -6 to 6
- values: bfloat16 [16384, 4096], P('ctx', 'chan'), may hold values from -0.15625 to 0.15625
- gate: bfloat16 [16384, 4096], P('ctx', 'chan'), may hold values from -6 to 6
- pre_gate: bfloat16 [16384, 4096], P('ctx', 'chan'), may hold values from -6 to 6
- filter_spectrum: float32 [2, 32768, 4096], P(None, 'ctx', 'chan'), may hold values from -6 to 6
- skip: float32 [4096], P('chan'), may hold values from 0.5 to 1.5
Outputs:
- input_grad: float32 [16384, 4096], P('ctx', 'chan')
- gate_grad: bfloat16 [16384, 4096], P('ctx', 'chan')
- filter_grad: float32 [16384, 4096], P('ctx', 'chan')
The draws below stay inside these ranges and needn't reach their ends.
All inputs are finite; a program needn't handle non-finite values.
Results may differ from the reference program's by a relative error of at most 0.0035.
Values may be sent and summed in bfloat16 or wider, within the bound.
A program may use at most 256 MiB of HBM per device.

```python
import jax
import jax.numpy as jnp
from jax import lax

CHANNELS = 4096
SEQ = 16384
FREQS = 32768


def levels(own_key, extent, split, low, largest):
    level = 1.0
    for dim, blocks in split:
        steps = jax.random.uniform(jax.random.fold_in(jax.random.fold_in(own_key, 6), dim), (blocks,), jnp.float32, low / len(split), largest / len(split))
        level = level * jnp.repeat(jnp.exp(steps), extent[dim] // blocks).reshape((-1,) + (1,) * (len(extent) - 1 - dim))
    return level


def noise(own_key, shape, spread, reach, cuts=(), dtype=jnp.bfloat16):
    level = levels(own_key, shape, cuts, -0.22, 0.18) if cuts else 1.0
    values = jax.random.normal(own_key, shape, jnp.float32) * spread * level
    return jnp.minimum(jnp.maximum(values, -reach), reach).astype(dtype)


def setup_inputs(seed: int = 0) -> dict:
    streams_of = jax.random.split(jax.random.key(seed), 7)
    return {
        "grad_out": noise(streams_of[0], (SEQ, CHANNELS), 1.0, 6.0, ((0, 8), (1, 16))),
        "values": noise(streams_of[1], (SEQ, CHANNELS), ((2.0 / SEQ) ** 0.5), 0.15625, ((0, 8), (1, 16))),
        "gate": noise(streams_of[2], (SEQ, CHANNELS), 1.0, 6.0, ((0, 8), (1, 16))),
        "pre_gate": noise(streams_of[3], (SEQ, CHANNELS), 1.0, 6.0, ((0, 8), (1, 16))),
        "filter_spectrum": noise(streams_of[4], (2, FREQS, CHANNELS), 0.7, 6.0, ((1, 8), (2, 16)), jnp.float32),
        "skip": jnp.clip(0.5 + 1.0 * jax.random.uniform(streams_of[5], (CHANNELS,), jnp.float32) ** levels(streams_of[5], (CHANNELS,), ((0, 16),), -0.2, 0.2), 0.5, 1.5),
    }


def one_block(pieces):
    grad_block, value_block, gate_block, spec_block, skip_block = pieces
    dy_block = grad_block.astype(jnp.float32) * gate_block.astype(jnp.float32)
    spec_dy = jnp.fft.fft(dy_block, n=FREQS, axis=0)
    spec_val = jnp.fft.fft(value_block.astype(jnp.float32), n=FREQS, axis=0)
    spec_filt = lax.complex(spec_block[0], spec_block[1])
    conv_part = jnp.real(jnp.fft.ifft(jnp.conj(spec_filt) * spec_dy, axis=0))[:SEQ]
    filt_part = jnp.real(jnp.fft.ifft(jnp.conj(spec_val) * spec_dy, axis=0))[:SEQ]
    return conv_part + skip_block[None, :] * dy_block, filt_part


def reference(grad_out, values, gate, pre_gate, filter_spectrum, skip):
    width = 256 if CHANNELS % 256 == 0 else CHANNELS
    blocks = CHANNELS // width

    def split_rows(array):
        return jnp.moveaxis(array.reshape(SEQ, blocks, width), 1, 0)

    spec_blocks = jnp.moveaxis(filter_spectrum.reshape(2, FREQS, blocks, width), 2, 0)
    skip_blocks = skip.reshape(blocks, width)
    input_blocks, filter_blocks = lax.map(one_block, (split_rows(grad_out), split_rows(values), split_rows(gate), spec_blocks, skip_blocks))
    input_grad = jnp.moveaxis(input_blocks, 0, 1).reshape(SEQ, CHANNELS)
    filter_grad = jnp.moveaxis(filter_blocks, 0, 1).reshape(SEQ, CHANNELS)
    gate_grad = (grad_out.astype(jnp.float32) * pre_gate.astype(jnp.float32)).astype(jnp.bfloat16)
    return input_grad, gate_grad, filter_grad
```

```python
import math
import functools
import numpy as np
import jax
import jax.numpy as jnp
import ml_dtypes
from jax import lax
from jax.experimental import pallas as pl
from jax.experimental.pallas import tpu as pltpu

F32 = jnp.float32
BF16 = jnp.bfloat16
N = 32768
LANE_KR = (0, 2, 1, 3)


def split_np(a):
    hi = a.astype(ml_dtypes.bfloat16)
    lo = (a - hi.astype(np.float64)).astype(ml_dtypes.bfloat16)
    return hi, lo


def tables():
    s = np.arange(512)
    ang = 2 * np.pi * ((s[:, None] * s[None, :]) % 512) / 512
    t = np.concatenate([np.cos(ang), np.sin(ang)], 0)
    hi, lo = split_np(t)
    kap = np.arange(9)[:, None] + 16 * np.array(LANE_KR)[None, :]
    prod = (kap[:, None, :] * s[None, :, None]) % N
    ang = 2 * np.pi * prod / N
    tw = np.concatenate([np.repeat(np.cos(ang), 32, 2), np.repeat(np.sin(ang), 32, 2)], 2).astype(np.float32)
    r = np.repeat(np.arange(4), 32)
    ang = 2 * np.pi * np.arange(9)[:, None] * r[None, :] / 64
    lane = np.stack([np.cos(ang), np.sin(ang)], 1).astype(np.float32)
    rev = np.eye(64)[::-1].astype(ml_dtypes.bfloat16)
    return hi, lo, tw, lane, rev


def lane_consts(rows):
    lanes = lax.broadcasted_iota(jnp.int32, (rows, 128), 1)
    block = lanes // 32
    hi = block >= 2
    odd = (block % 2) == 1
    last = block == 3
    return hi, odd, last


def pair64(x, hi):
    return pltpu.roll(x, 64, 1) + jnp.where(hi, -x, x)


def pair32(x, odd):
    return jnp.where(odd, pltpu.roll(x, 32, 1) - x, x + pltpu.roll(x, 96, 1))


def dft4(re, im, masks):
    hi, odd, last = masks
    re, im = pair64(re, hi), pair64(im, hi)
    re, im = jnp.where(last, im, re), jnp.where(last, -re, im)
    return pair32(re, odd), pair32(im, odd)


def idft4(re, im, masks):
    hi, odd, last = masks
    re, im = pair32(re, odd), pair32(im, odd)
    re, im = jnp.where(last, -im, re), jnp.where(last, re, im)
    return pair64(re, hi), pair64(im, hi)


C = [math.cos(2 * math.pi * q / 16) for q in range(16)]
S = [math.sin(2 * math.pi * q / 16) for q in range(16)]


def dft16_half(x):
    y = [None] * 9
    e = [x[i] + x[i + 4] for i in range(4)]
    f = [x[i] - x[i + 4] for i in range(4)]
    a, b = e[0] + e[2], e[1] + e[3]
    y[0] = (a + b, None)
    y[8] = (a - b, None)
    y[4] = (e[0] - e[2], e[3] - e[1])
    g, h = C[2] * (f[1] - f[3]), C[2] * (f[1] + f[3])
    y[2] = (f[0] + g, -(f[2] + h))
    y[6] = (f[0] - g, f[2] - h)
    d = [None] + [x[i] - x[8 - i] for i in (1, 2, 3)]
    s = [None] + [x[i] + x[8 - i] for i in (1, 2, 3)]
    for k in (1, 3):
        p = x[0] + d[2] * C[2 * k % 16]
        q = d[1] * C[k] + d[3] * C[3 * k % 16]
        u = s[1] * S[k] + s[3] * S[3 * k % 16]
        v = s[2] * S[2 * k % 16] + x[4] * S[4 * k % 16]
        y[k] = (p + q, -(u + v))
        y[8 - k] = (p - q, v - u)
    return y


def idft16_half(z):
    a, b = z[0][0] + z[8][0], z[0][0] - z[8][0]
    r4, i4 = z[4]
    e = [a + r4, b - i4, a - r4, b + i4]
    (r2, i2), (r6, i6) = z[2], z[6]
    m, n = r2 - r6, i2 + i6
    f = [r2 + r6, C[2] * (m - n), i6 - i2, -C[2] * (m + n)]
    out = [e[i] + f[i] for i in range(4)] + [e[i] - f[i] for i in range(4)]
    u = [0.0] * 5
    v = [0.0] * 5
    for k in (1, 3):
        rp, rm = z[k][0] + z[8 - k][0], z[k][0] - z[8 - k][0]
        ip, im = z[k][1] + z[8 - k][1], z[k][1] - z[8 - k][1]
        u[0] = u[0] + rp
        v[4] = v[4] + im * S[4 * k % 16]
        for q in (1, 2, 3):
            odd = q % 2 == 1
            u[q] = u[q] + (rm if odd else rp) * C[q * k % 16]
            v[q] = v[q] + (ip if odd else im) * S[q * k % 16]
    out[0] = out[0] + u[0]
    out[4] = out[4] - v[4]
    for q in (1, 2, 3):
        out[q] = out[q] + u[q] - v[q]
        out[8 - q] = out[8 - q] - u[q] - v[q]
    return out


TILE = 16


def fwd_vector(x_ref, u_ref, tw_ref, lane_ref):
    masks = lane_consts(TILE)

    def step(i, _):
        row = pl.multiple_of(i * TILE, TILE)
        rows = pl.ds(row, TILE)
        low = pl.ds(row + 512, TILE)
        y = dft16_half([x_ref[q, rows, :].astype(F32) for q in range(8)])
        for k in range(9):
            re, im = y[k]
            if k:
                lc, ls = lane_ref[k, 0:1, :], lane_ref[k, 1:2, :]
                if im is None:
                    re, im = re * lc, -(re * ls)
                else:
                    re, im = re * lc + im * ls, im * lc - re * ls
            else:
                im = jnp.zeros_like(re)
            re, im = dft4(re, im, masks)
            tc, ts = tw_ref[k, rows, 0:128], tw_ref[k, rows, 128:256]
            re, im = re * tc + im * ts, im * tc - re * ts
            for part, at in ((re, 0), (im, 128)):
                high = part.astype(BF16)
                u_ref[k, rows, at : at + 128] = high
                u_ref[k, low, at : at + 128] = (part - high.astype(F32)).astype(BF16)
        return 0

    lax.fori_loop(0, 512 // TILE, step, 0)


def inv_vector(z_ref, tw_ref, lane_ref, emit, edge, scale):
    masks = lane_consts(TILE)

    def step(i, _):
        row = pl.multiple_of(i * TILE, TILE)
        rows = pl.ds(row, TILE)
        z = []
        for k in range(9):
            re, im = z_ref[k, rows, 0:128], z_ref[k, rows, 128:256]
            tc, ts = tw_ref[k, rows, 0:128], tw_ref[k, rows, 128:256]
            re, im = re * tc - im * ts, im * tc + re * ts
            re, im = idft4(re, im, masks)
            if k:
                lc, ls = lane_ref[k, 0:1, :], lane_ref[k, 1:2, :]
                re, im = re * lc - im * ls, im * lc + re * ls
            if k in (0, 8) and edge != 1.0:
                re = re * edge
            z.append((re, im))
        for q, value in enumerate(idft16_half(z)):
            emit(rows, q, value * scale)
        return 0

    lax.fori_loop(0, 512 // TILE, step, 0)


def matrix_stage(hi_ref, lo_ref, data):
    out = jnp.dot(hi_ref[...], data[...], preferred_element_type=F32)
    out = out + jnp.dot(lo_ref[...], data[0:512, :], preferred_element_type=F32)
    return out


def forward_block(hi_ref, lo_ref, u):
    out = matrix_stage(hi_ref, lo_ref, u)
    c, s = out[0:512], out[512:1024]
    return c[:, 0:128] + s[:, 128:256], c[:, 128:256] - s[:, 0:128]


def inverse_block(hi_ref, lo_ref, g_ref):
    out = matrix_stage(hi_ref, lo_ref, g_ref)
    c, s = out[0:512], out[512:1024]
    return c[:, 0:128] - s[:, 128:256], c[:, 128:256] + s[:, 0:128]


def put_split(ref, re, im):
    for part, at in ((re, 0), (im, 128)):
        high = part.astype(BF16)
        ref[0:512, at : at + 128] = high
        ref[512:1024, at : at + 128] = (part - high.astype(F32)).astype(BF16)


def corr_kernel(dy_ref, v_ref, hi_ref, lo_ref, tw_ref, lane_ref, spec_ref, out_ref, u_ref, z_ref, g_ref):
    fwd_vector(dy_ref, u_ref.at[0], tw_ref, lane_ref)
    fwd_vector(v_ref, u_ref.at[1], tw_ref, lane_ref)

    def block(k, _):
        dr, di = forward_block(hi_ref, lo_ref, u_ref.at[0, k])
        spec_ref[k, :, 0:128] = dr
        spec_ref[k, :, 128:256] = di
        vr, vi = forward_block(hi_ref, lo_ref, u_ref.at[1, k])
        put_split(g_ref, vr * dr + vi * di, vr * di - vi * dr)
        zr, zi = inverse_block(hi_ref, lo_ref, g_ref)
        z_ref[k, :, 0:128] = zr
        z_ref[k, :, 128:256] = zi
        return 0

    lax.fori_loop(0, 9, block, 0)

    def emit(rows, q, value):
        out_ref[q, rows, :] = value.astype(BF16)

    inv_vector(z_ref, tw_ref, lane_ref, emit, 0.5, 2.0 / N)


def conv_kernel(spec_ref, h_ref, hi_ref, lo_ref, tw_ref, lane_ref, out_ref, z_ref, g_ref):
    def block(k, _):
        mirror = jnp.where(k == 0, 0, 16 - k)
        both = jnp.where((k == 0) | (k == 8), 0.0, 1.0)
        for p in range(8):
            rows = pl.ds(64 * p, 64)
            low = pl.ds(512 + 64 * p, 64)
            mr = h_ref[7 - p, 0, mirror].astype(F32) * both
            mi = h_ref[7 - p, 1, mirror].astype(F32) * both
            hr = h_ref[p, 0, k].astype(F32) + mr
            hi = h_ref[p, 1, k].astype(F32) - mi
            dr, di = spec_ref[k, rows, 0:128], spec_ref[k, rows, 128:256]
            for part, at in ((hr * dr + hi * di, 0), (hr * di - hi * dr, 128)):
                high = part.astype(BF16)
                g_ref[rows, at : at + 128] = high
                g_ref[low, at : at + 128] = (part - high.astype(F32)).astype(BF16)
        zr, zi = inverse_block(hi_ref, lo_ref, g_ref)
        z_ref[k, :, 0:128] = zr
        z_ref[k, :, 128:256] = zi
        return 0

    lax.fori_loop(0, 9, block, 0)

    def emit(rows, q, value):
        out_ref[q, rows, :] = value.astype(BF16)

    inv_vector(z_ref, tw_ref, lane_ref, emit, 1.0, 1.0 / N)


def swap_blocks(blocks):
    rows = blocks[0].shape[0]
    hi, odd, _ = lane_consts(rows)
    b = list(blocks)
    for i in (0, 1):
        x, y = b[i], b[i + 2]
        b[i] = jnp.where(hi, pltpu.roll(y, 64, 1), x)
        b[i + 2] = jnp.where(hi, y, pltpu.roll(x, 64, 1))
    for i in (0, 2):
        x, y = b[i], b[i + 1]
        b[i] = jnp.where(odd, pltpu.roll(y, 32, 1), x)
        b[i + 1] = jnp.where(odd, y, pltpu.roll(x, 96, 1))
    return b


def pack_tokens_kernel(grad_ref, gate_ref, val_ref, out_ref):
    def step(i, _):
        row = pl.multiple_of(i * TILE, TILE)
        for half in range(2):
            lanes = slice(128 * half, 128 * half + 128)
            at = [pl.ds(512 * r + row, TILE) for r in range(4)]
            dy = [grad_ref[a, lanes].astype(F32) * gate_ref[a, lanes].astype(F32) for a in at]
            va = [val_ref[a, lanes].astype(F32) for a in at]
            for j, group in enumerate((dy, va)):
                for e, value in enumerate(swap_blocks(group)):
                    out_ref[4 * half + e, j, pl.ds(row, TILE), :] = value.astype(BF16)
        return 0

    lax.fori_loop(0, 512 // TILE, step, 0)


def pack_spectrum_kernel(hbm_ref, rev_ref, out_ref, h_ref, sems):
    copies = [
        pltpu.make_async_copy(hbm_ref.at[ri, :, pl.ds(128 * half, 128)], h_ref.at[ri, half], sems.at[ri, half])
        for ri in range(2)
        for half in range(2)
    ]
    for c in copies:
        c.start()
    for c in copies:
        c.wait()

    def plain(kq, _):
        for ri in range(2):
            for half in range(2):
                blocks = [h_ref[ri, half, pl.ds(kq + 16 * kr, 64, stride=64), :] for kr in LANE_KR]
                for e, value in enumerate(swap_blocks(blocks)):
                    out_ref[4 * half + e, ri, kq] = value.astype(BF16)
        return 0

    def mirrored(kq, _):
        for ri in range(2):
            for half in range(2):
                blocks = [h_ref[ri, half, pl.ds(kq + 16 * kr, 64, stride=64), :] for kr in LANE_KR[::-1]]
                wide = jnp.concatenate([value.astype(BF16) for value in swap_blocks(blocks)], 1)
                wide = jnp.dot(rev_ref[...], wide, preferred_element_type=F32).astype(BF16)
                for e in range(4):
                    out_ref[4 * half + e, ri, kq] = wide[:, 128 * e : 128 * e + 128]
        return 0

    lax.fori_loop(0, 9, plain, 0)
    lax.fori_loop(9, 16, mirrored, 0)


def unpack_kernel(conv_ref, corr_ref, grad_ref, gate_ref, pre_ref, skip_ref, in_ref, gg_ref, fg_ref):
    def step(i, _):
        row = pl.multiple_of(i * TILE, TILE)
        for half in range(2):
            lanes = slice(128 * half, 128 * half + 128)
            at = [pl.ds(512 * r + row, TILE) for r in range(4)]
            conv = swap_blocks([conv_ref[4 * half + e, pl.ds(row, TILE), :].astype(F32) for e in range(4)])
            corr = swap_blocks([corr_ref[4 * half + e, pl.ds(row, TILE), :].astype(F32) for e in range(4)])
            skip = skip_ref[:, lanes]
            for r in range(4):
                g = grad_ref[at[r], lanes].astype(F32)
                in_ref[at[r], lanes] = conv[r] + skip * (g * gate_ref[at[r], lanes].astype(F32))
                gg_ref[at[r], lanes] = (g * pre_ref[at[r], lanes].astype(F32)).astype(BF16)
                fg_ref[at[r], lanes] = corr[r]
        return 0

    lax.fori_loop(0, 512 // TILE, step, 0)


VMEM = pl.BlockSpec(memory_space=pltpu.VMEM)
PARAMS = pltpu.CompilerParams(vmem_limit_bytes=56 << 20)


def call(body, outs, ins, scratch=(), anys=()):
    return pl.pallas_call(
        body,
        out_shape=outs,
        in_specs=[pl.BlockSpec(memory_space=pl.ANY) if i in anys else VMEM for i in range(len(ins))],
        out_specs=jax.tree.map(lambda _: VMEM, outs),
        scratch_shapes=list(scratch),
        compiler_params=PARAMS,
    )(*ins)


def on_device(grad_out, values, gate, pre_gate, filter_spectrum, skip):
    S_ = jax.ShapeDtypeStruct
    hi, lo, tw, lane, rev = tables()
    hi2 = jnp.asarray(np.concatenate([hi, hi], 1))
    lo, tw, lane, rev = (jnp.asarray(a) for a in (lo, tw, lane, rev))
    tokens = call(pack_tokens_kernel, S_((8, 2, 512, 128), BF16), (grad_out, gate, values))
    tokens = lax.all_to_all(tokens, "ctx", 0, 0, tiled=True)
    packed = call(pack_spectrum_kernel, S_((8, 2, 16, 64, 128), BF16), (filter_spectrum, rev),
        (pltpu.VMEM((2, 2, 4096, 128), F32), pltpu.SemaphoreType.DMA((2, 2))), (0,))
    spectrum = lax.all_to_all(packed, "ctx", 0, 0, tiled=True)
    spec, corr = call(
        corr_kernel,
        (S_((9, 512, 256), F32), S_((8, 512, 128), BF16)),
        (tokens[:, 0], tokens[:, 1], hi2, lo, tw, lane),
        (pltpu.VMEM((2, 9, 1024, 256), BF16), pltpu.VMEM((9, 512, 256), F32), pltpu.VMEM((1024, 256), BF16)),
    )
    corr = lax.all_to_all(corr, "ctx", 0, 0, tiled=True)
    conv = call(
        conv_kernel,
        S_((8, 512, 128), BF16),
        (spec, spectrum, hi2, lo, tw, lane),
        (pltpu.VMEM((9, 512, 256), F32), pltpu.VMEM((1024, 256), BF16)),
    )
    conv = lax.all_to_all(conv, "ctx", 0, 0, tiled=True)
    return tuple(
        call(
            unpack_kernel,
            (S_((2048, 256), F32), S_((2048, 256), BF16), S_((2048, 256), F32)),
            (conv, corr, grad_out, gate, pre_gate, skip.reshape(1, 256)),
        )
    )


def solution(mesh):
    from jax.sharding import PartitionSpec as P
    rows = P("ctx", "chan")
    return jax.shard_map(
        on_device,
        mesh=mesh,
        in_specs=(rows, rows, rows, rows, P(None, "ctx", "chan"), P("chan")),
        out_specs=(rows, rows, rows),
        check_vma=False,
    )
```

```python
import math
import functools
import numpy as np
import jax
import jax.numpy as jnp
import ml_dtypes
from jax import lax
from jax.sharding import PartitionSpec as P
from jax.experimental import pallas as pl
from jax.experimental.pallas import tpu as pltpu

F32 = jnp.float32
BF16 = jnp.bfloat16
N = 32768
LANE_KR = (0, 2, 1, 3)


def split_np(a):
    hi = a.astype(ml_dtypes.bfloat16)
    lo = (a - hi.astype(np.float64)).astype(ml_dtypes.bfloat16)
    return hi, lo


def tables():
    s = np.arange(512)
    ang = 2 * np.pi * ((s[:, None] * s[None, :]) % 512) / 512
    t = np.concatenate([np.cos(ang), np.sin(ang)], 0)
    hi, lo = split_np(t)
    kap = np.arange(9)[:, None] + 16 * np.array(LANE_KR)[None, :]
    prod = (kap[:, None, :] * s[None, :, None]) % N
    ang = 2 * np.pi * prod / N
    tw = np.concatenate([np.repeat(np.cos(ang), 32, 2), np.repeat(np.sin(ang), 32, 2)], 2).astype(np.float32)
    r = np.repeat(np.arange(4), 32)
    ang = 2 * np.pi * np.arange(9)[:, None] * r[None, :] / 64
    lane = np.stack([np.cos(ang), np.sin(ang)], 1).astype(np.float32)
    rev = np.eye(64)[::-1].astype(ml_dtypes.bfloat16)
    return hi, lo, tw, lane, rev


def lane_consts(rows):
    lanes = lax.broadcasted_iota(jnp.int32, (rows, 128), 1)
    block = lanes // 32
    hi = block >= 2
    odd = (block % 2) == 1
    last = block == 3
    return hi, odd, last


def pair64(x, hi):
    return pltpu.roll(x, 64, 1) + jnp.where(hi, -x, x)


def pair32(x, odd):
    return jnp.where(odd, pltpu.roll(x, 32, 1) - x, x + pltpu.roll(x, 96, 1))


def dft4(re, im, masks):
    hi, odd, last = masks
    re, im = pair64(re, hi), pair64(im, hi)
    re, im = jnp.where(last, im, re), jnp.where(last, -re, im)
    return pair32(re, odd), pair32(im, odd)


def idft4(re, im, masks):
    hi, odd, last = masks
    re, im = pair32(re, odd), pair32(im, odd)
    re, im = jnp.where(last, -im, re), jnp.where(last, re, im)
    return pair64(re, hi), pair64(im, hi)


C = [math.cos(2 * math.pi * q / 16) for q in range(16)]
S = [math.sin(2 * math.pi * q / 16) for q in range(16)]


def dft16_half(x):
    y = [None] * 9
    e = [x[i] + x[i + 4] for i in range(4)]
    f = [x[i] - x[i + 4] for i in range(4)]
    a, b = e[0] + e[2], e[1] + e[3]
    y[0] = (a + b, None)
    y[8] = (a - b, None)
    y[4] = (e[0] - e[2], e[3] - e[1])
    g, h = C[2] * (f[1] - f[3]), C[2] * (f[1] + f[3])
    y[2] = (f[0] + g, -(f[2] + h))
    y[6] = (f[0] - g, f[2] - h)
    d = [None] + [x[i] - x[8 - i] for i in (1, 2, 3)]
    s = [None] + [x[i] + x[8 - i] for i in (1, 2, 3)]
    for k in (1, 3):
        p = x[0] + d[2] * C[2 * k % 16]
        q = d[1] * C[k] + d[3] * C[3 * k % 16]
        u = s[1] * S[k] + s[3] * S[3 * k % 16]
        v = s[2] * S[2 * k % 16] + x[4] * S[4 * k % 16]
        y[k] = (p + q, -(u + v))
        y[8 - k] = (p - q, v - u)
    return y


def idft16_half(z):
    a, b = z[0][0] + z[8][0], z[0][0] - z[8][0]
    r4, i4 = z[4]
    e = [a + r4, b - i4, a - r4, b + i4]
    (r2, i2), (r6, i6) = z[2], z[6]
    m, n = r2 - r6, i2 + i6
    f = [r2 + r6, C[2] * (m - n), i6 - i2, -C[2] * (m + n)]
    out = [e[i] + f[i] for i in range(4)] + [e[i] - f[i] for i in range(4)]
    u = [0.0] * 5
    v = [0.0] * 5
    for k in (1, 3):
        rp, rm = z[k][0] + z[8 - k][0], z[k][0] - z[8 - k][0]
        ip, im = z[k][1] + z[8 - k][1], z[k][1] - z[8 - k][1]
        u[0] = u[0] + rp
        v[4] = v[4] + im * S[4 * k % 16]
        for q in (1, 2, 3):
            odd = q % 2 == 1
            u[q] = u[q] + (rm if odd else rp) * C[q * k % 16]
            v[q] = v[q] + (ip if odd else im) * S[q * k % 16]
    out[0] = out[0] + u[0]
    out[4] = out[4] - v[4]
    for q in (1, 2, 3):
        out[q] = out[q] + u[q] - v[q]
        out[8 - q] = out[8 - q] - u[q] - v[q]
    return out


TILE = 16


def fwd_vector(x_ref, u_ref, tw_ref, lane_ref):
    masks = lane_consts(TILE)

    def step(i, _):
        row = pl.multiple_of(i * TILE, TILE)
        rows = pl.ds(row, TILE)
        low = pl.ds(row + 512, TILE)
        y = dft16_half([x_ref[q, rows, :].astype(F32) for q in range(8)])
        for k in range(9):
            re, im = y[k]
            if k:
                lc, ls = lane_ref[k, 0:1, :], lane_ref[k, 1:2, :]
                if im is None:
                    re, im = re * lc, -(re * ls)
                else:
                    re, im = re * lc + im * ls, im * lc - re * ls
            else:
                im = jnp.zeros_like(re)
            re, im = dft4(re, im, masks)
            tc, ts = tw_ref[k, rows, 0:128], tw_ref[k, rows, 128:256]
            re, im = re * tc + im * ts, im * tc - re * ts
            for part, at in ((re, 0), (im, 128)):
                high = part.astype(BF16)
                u_ref[k, rows, at : at + 128] = high
                u_ref[k, low, at : at + 128] = (part - high.astype(F32)).astype(BF16)
        return 0

    lax.fori_loop(0, 512 // TILE, step, 0)


def inv_vector(z_ref, tw_ref, lane_ref, emit, edge, scale):
    masks = lane_consts(TILE)

    def step(i, _):
        row = pl.multiple_of(i * TILE, TILE)
        rows = pl.ds(row, TILE)
        z = []
        for k in range(9):
            re = z_ref[pl.ds(1024 * k + row, TILE), :]
            im = z_ref[pl.ds(1024 * k + 512 + row, TILE), :]
            tc, ts = tw_ref[k, rows, 0:128], tw_ref[k, rows, 128:256]
            re, im = re * tc - im * ts, im * tc + re * ts
            re, im = idft4(re, im, masks)
            if k:
                lc, ls = lane_ref[k, 0:1, :], lane_ref[k, 1:2, :]
                re, im = re * lc - im * ls, im * lc + re * ls
            if k in (0, 8) and edge != 1.0:
                re = re * edge
            z.append((re, im))
        for q, value in enumerate(idft16_half(z)):
            emit(rows, q, value * scale)
        return 0

    lax.fori_loop(0, 512 // TILE, step, 0)


def matrix_stage(hi_ref, lo_ref, data):
    out = jnp.dot(hi_ref[...], data[...], preferred_element_type=F32)
    out = out + jnp.dot(lo_ref[...], data[0:512, :], preferred_element_type=F32)
    return out


def forward_block(hi_ref, lo_ref, u):
    out = matrix_stage(hi_ref, lo_ref, u)
    c, s = out[0:512], out[512:1024]
    return c[:, 0:128] + s[:, 128:256], c[:, 128:256] - s[:, 0:128]


def inverse_block(hi_ref, lo_ref, g_ref):
    out = matrix_stage(hi_ref, lo_ref, g_ref)
    c, s = out[0:512], out[512:1024]
    return c[:, 0:128] - s[:, 128:256], c[:, 128:256] + s[:, 0:128]


def put_split(ref, re, im):
    for part, at in ((re, 0), (im, 128)):
        high = part.astype(BF16)
        ref[0:512, at : at + 128] = high
        ref[512:1024, at : at + 128] = (part - high.astype(F32)).astype(BF16)


def swap_blocks(blocks):
    rows = blocks[0].shape[0]
    hi, odd, _ = lane_consts(rows)
    b = list(blocks)
    for i in (0, 1):
        x, y = b[i], b[i + 2]
        b[i] = jnp.where(hi, pltpu.roll(y, 64, 1), x)
        b[i + 2] = jnp.where(hi, y, pltpu.roll(x, 64, 1))
    for i in (0, 2):
        x, y = b[i], b[i + 1]
        b[i] = jnp.where(odd, pltpu.roll(y, 32, 1), x)
        b[i + 1] = jnp.where(odd, y, pltpu.roll(x, 96, 1))
    return b


def unpack_kernel(conv_ref, corr_ref, grad_ref, gate_ref, pre_ref, skip_ref, in_ref, gg_ref, fg_ref):
    def step(i, _):
        row = pl.multiple_of(i * TILE, TILE)
        for half in range(2):
            lanes = slice(128 * half, 128 * half + 128)
            at = [pl.ds(512 * r + row, TILE) for r in range(4)]
            conv = swap_blocks([conv_ref[4 * half + e, pl.ds(row, TILE), :].astype(F32) for e in range(4)])
            corr = swap_blocks([corr_ref[4 * half + e, pl.ds(row, TILE), :].astype(F32) for e in range(4)])
            skip = skip_ref[:, lanes]
            for r in range(4):
                g = grad_ref[at[r], lanes].astype(F32)
                in_ref[at[r], lanes] = conv[r] + skip * (g * gate_ref[at[r], lanes].astype(F32))
                gg_ref[at[r], lanes] = (g * pre_ref[at[r], lanes].astype(F32)).astype(BF16)
                fg_ref[at[r], lanes] = corr[r]
        return 0

    lax.fori_loop(0, 512 // TILE, step, 0)


VMEM = pl.BlockSpec(memory_space=pltpu.VMEM)
PARAMS = pltpu.CompilerParams(vmem_limit_bytes=56 << 20)


def call(body, outs, ins, scratch=(), anys=()):
    return pl.pallas_call(
        body,
        out_shape=outs,
        in_specs=[pl.BlockSpec(memory_space=pl.ANY) if i in anys else VMEM for i in range(len(ins))],
        out_specs=jax.tree.map(lambda _: VMEM, outs),
        scratch_shapes=list(scratch),
        compiler_params=PARAMS,
    )(*ins)


MESH = pl.DeviceIdType.MESH
OFFSETS = ((2, 1), (2, 0), (1, 1), (3, 1), (1, 0), (3, 0), (0, 1))
SLOT = {}
for _i, _k in enumerate((0, 8, 1, 15, 2, 14, 3, 13, 4, 12, 5, 11, 6, 10, 7, 9)):
    SLOT[_k] = _i
SPEC = 9 * 1024


def pack_dy(grad_ref, gate_ref, out_ref):
    def step(i, _):
        row = pl.multiple_of(i * TILE, TILE)
        for half in range(2):
            lanes = slice(128 * half, 128 * half + 128)
            at = [pl.ds(512 * r + row, TILE) for r in range(4)]
            dy = [grad_ref[a, lanes].astype(F32) * gate_ref[a, lanes].astype(F32) for a in at]
            for e, value in enumerate(swap_blocks(dy)):
                out_ref[4 * half + e, pl.ds(row, TILE), :] = value.astype(BF16)
        return 0

    lax.fori_loop(0, 512 // TILE, step, 0)


def pack_values(val_ref, out_ref):
    def step(i, _):
        row = pl.multiple_of(i * TILE, TILE)
        for half in range(2):
            lanes = slice(128 * half, 128 * half + 128)
            va = [val_ref[pl.ds(512 * r + row, TILE), lanes].astype(F32) for r in range(4)]
            for e, value in enumerate(swap_blocks(va)):
                out_ref[4 * half + e, pl.ds(row, TILE), :] = value.astype(BF16)
        return 0

    lax.fori_loop(0, 512 // TILE, step, 0)


def pack_plain(h_ref, out_ref, kq, slot):
    for ri in range(2):
        for half in range(2):
            base = (2 * ri + half) * 4096 + kq
            blocks = [h_ref[pl.ds(base + 16 * kr, 64, stride=64), :] for kr in LANE_KR]
            for e, value in enumerate(swap_blocks(blocks)):
                out_ref[4 * half + e, slot, ri] = value.astype(BF16)


def pack_mirrored(h_ref, rev_ref, out_ref, kq, slot):
    for ri in range(2):
        for half in range(2):
            base = (2 * ri + half) * 4096 + kq
            blocks = [h_ref[pl.ds(base + 16 * kr, 64, stride=64), :] for kr in LANE_KR[::-1]]
            wide = jnp.concatenate([value.astype(BF16) for value in swap_blocks(blocks)], 1)
            wide = jnp.dot(rev_ref[...], wide, preferred_element_type=F32).astype(BF16)
            for e in range(4):
                out_ref[4 * half + e, slot, ri] = wide[:, 128 * e : 128 * e + 128]


def pack_spectrum(h_ref, rev_ref, out_ref, chunk):
    if chunk == 0:
        pack_plain(h_ref, out_ref, 0, 0)
        pack_plain(h_ref, out_ref, 8, 1)
        pack_plain(h_ref, out_ref, 1, 2)
        pack_mirrored(h_ref, rev_ref, out_ref, 15, 3)
        return

    def step(i, _):
        k = 2 * chunk + i
        pack_plain(h_ref, out_ref, k, 4 * chunk + 2 * i)
        pack_mirrored(h_ref, rev_ref, out_ref, 16 - k, 4 * chunk + 2 * i + 1)
        return 0

    lax.fori_loop(0, 2, step, 0)


def conv_block(big_ref, h_ref, hi_ref, lo_ref, g_ref, k, slot, mirror):
    for p in range(8):
        rows = pl.ds(64 * p, 64)
        low = pl.ds(512 + 64 * p, 64)
        hr = h_ref[p, slot, 0].astype(F32)
        hi = h_ref[p, slot, 1].astype(F32)
        if mirror is not None:
            hr = hr + h_ref[7 - p, mirror, 0].astype(F32)
            hi = hi - h_ref[7 - p, mirror, 1].astype(F32)
        dr = big_ref[pl.ds(SPEC + 1024 * k + 64 * p, 64), :]
        di = big_ref[pl.ds(SPEC + 1024 * k + 512 + 64 * p, 64), :]
        for part, at in ((hr * dr + hi * di, 0), (hr * di - hi * dr, 128)):
            high = part.astype(BF16)
            g_ref[rows, at : at + 128] = high
            g_ref[low, at : at + 128] = (part - high.astype(F32)).astype(BF16)
    zr, zi = inverse_block(hi_ref, lo_ref, g_ref)
    big_ref[pl.ds(1024 * k, 512), :] = zr
    big_ref[pl.ds(1024 * k + 512, 512), :] = zi


def main_kernel(
    grad_hbm, gate_hbm, val_hbm, h_hbm, hi_hbm, lo_hbm, tw_hbm, lane_ref, rev_ref,
    corr_out, conv_out,
    grad_v, gate_v, val_v, hi_v, lo_v, tw_v, tok_send, tok_recv, h_send, h_recv,
    big, u_ref, g_ref, res_send, load_sems, own_sems, send_sems, recv_sems,
):
    me = lax.axis_index("ctx")
    x, z = me // 2, me % 2
    peers = [((x + dx) % 4) * 2 + (z + dz) % 2 for dx, dz in OFFSETS]

    loads = [(grad_hbm, grad_v), (gate_hbm, gate_v), (val_hbm, val_v)]
    for ri in range(2):
        for half in range(2):
            loads.append((h_hbm.at[ri, :, pl.ds(128 * half, 128)], big.at[pl.ds((2 * ri + half) * 4096, 4096), :]))
    loads += [(tw_hbm, tw_v), (hi_hbm, hi_v), (lo_hbm, lo_v)]
    loads = [pltpu.make_async_copy(a, b, load_sems.at[i]) for i, (a, b) in enumerate(loads)]
    for c in loads:
        c.start()
    barrier = pltpu.get_barrier_semaphore()
    for peer in peers:
        pl.semaphore_signal(barrier, inc=1, device_id={"ctx": peer}, device_id_type=MESH)

    def exchange(group, source, target):
        copies = []
        for i, peer in enumerate(peers):
            c = pltpu.make_async_remote_copy(
                src_ref=source(peer), dst_ref=target,
                send_sem=send_sems.at[group, i], recv_sem=recv_sems.at[group, i],
                device_id={"ctx": peer}, device_id_type=MESH,
            )
            c.start()
            copies.append(c)
        own = pltpu.make_async_copy(source(me), target, own_sems.at[group])
        own.start()
        return copies, own

    def arrived(pair):
        for c in pair[0]:
            c.wait_recv()
        pair[1].wait()

    loads[0].wait()
    loads[1].wait()
    pack_dy(grad_v, gate_v, tok_send.at[0])
    pl.semaphore_wait(barrier, 7)
    dy_move = exchange(0, lambda d: tok_send.at[0, d], tok_recv.at[0, me])
    loads[2].wait()
    pack_values(val_v, tok_send.at[1])
    val_move = exchange(1, lambda d: tok_send.at[1, d], tok_recv.at[1, me])
    for c in loads[3:7]:
        c.wait()
    h_moves = []
    for chunk in range(4):
        pack_spectrum(big, rev_ref, h_send, chunk)
        part = pl.ds(4 * chunk, 4)
        h_moves.append(exchange(2 + chunk, lambda d: h_send.at[d, part], h_recv.at[me, part]))
    for c in loads[7:]:
        c.wait()

    arrived(dy_move)
    fwd_vector(tok_recv.at[0], u_ref.at[0], tw_v, lane_ref)
    arrived(val_move)
    fwd_vector(tok_recv.at[1], u_ref.at[1], tw_v, lane_ref)

    def block(k, _):
        dr, di = forward_block(hi_v, lo_v, u_ref.at[0, k])
        big[pl.ds(SPEC + 1024 * k, 512), :] = dr
        big[pl.ds(SPEC + 1024 * k + 512, 512), :] = di
        vr, vi = forward_block(hi_v, lo_v, u_ref.at[1, k])
        put_split(g_ref, vr * dr + vi * di, vr * di - vi * dr)
        zr, zi = inverse_block(hi_v, lo_v, g_ref)
        big[pl.ds(1024 * k, 512), :] = zr
        big[pl.ds(1024 * k + 512, 512), :] = zi
        return 0

    lax.fori_loop(0, 9, block, 0)

    def emit_to(n):
        def emit(rows, q, value):
            res_send[n, q, rows, :] = value.astype(BF16)
        return emit

    inv_vector(big, tw_v, lane_ref, emit_to(0), 0.5, 2.0 / N)
    corr_move = exchange(6, lambda d: res_send.at[0, d], corr_out.at[me])

    for chunk in range(4):
        arrived(h_moves[chunk])
        if chunk == 0:
            conv_block(big, h_recv, hi_v, lo_v, g_ref, 0, 0, None)
            conv_block(big, h_recv, hi_v, lo_v, g_ref, 8, 1, None)
            conv_block(big, h_recv, hi_v, lo_v, g_ref, 1, 2, 3)
        else:
            def step(i, _, chunk=chunk):
                slot = 4 * chunk + 2 * i
                conv_block(big, h_recv, hi_v, lo_v, g_ref, 2 * chunk + i, slot, slot + 1)
                return 0
            lax.fori_loop(0, 2, step, 0)
    inv_vector(big, tw_v, lane_ref, emit_to(1), 1.0, 1.0 / N)
    conv_move = exchange(7, lambda d: res_send.at[1, d], conv_out.at[me])
    arrived(corr_move)
    arrived(conv_move)
    for pair in (dy_move, val_move, *h_moves, corr_move, conv_move):
        for c in pair[0]:
            c.wait_send()


def on_device(grad_out, values, gate, pre_gate, filter_spectrum, skip):
    S_ = jax.ShapeDtypeStruct
    hi, lo, tw, lane, rev = tables()
    hi2 = jnp.asarray(np.concatenate([hi, hi], 1))
    lo, tw, lane, rev = (jnp.asarray(a) for a in (lo, tw, lane, rev))
    anywhere = pl.BlockSpec(memory_space=pl.ANY)
    result = S_((8, 512, 128), BF16)
    corr, conv = pl.pallas_call(
        main_kernel,
        out_shape=(result, result),
        in_specs=[anywhere] * 7 + [VMEM] * 2,
        out_specs=(anywhere, anywhere),
        scratch_shapes=[
            pltpu.VMEM((2048, 256), BF16),
            pltpu.VMEM((2048, 256), BF16),
            pltpu.VMEM((2048, 256), BF16),
            pltpu.VMEM((1024, 1024), BF16),
            pltpu.VMEM((1024, 512), BF16),
            pltpu.VMEM((9, 512, 256), F32),
            pltpu.VMEM((2, 8, 512, 128), BF16),
            pltpu.VMEM((2, 8, 512, 128), BF16),
            pltpu.VMEM((8, 16, 2, 64, 128), BF16),
            pltpu.VMEM((8, 16, 2, 64, 128), BF16),
            pltpu.VMEM((18 * 1024, 128), F32),
            pltpu.VMEM((2, 9, 1024, 256), BF16),
            pltpu.VMEM((1024, 256), BF16),
            pltpu.VMEM((2, 8, 512, 128), BF16),
            pltpu.SemaphoreType.DMA((10,)),
            pltpu.SemaphoreType.DMA((8,)),
            pltpu.SemaphoreType.DMA((8, 7)),
            pltpu.SemaphoreType.DMA((8, 7)),
        ],
        compiler_params=pltpu.CompilerParams(collective_id=0, has_side_effects=True, vmem_limit_bytes=58 << 20),
    )(grad_out, gate, values, filter_spectrum, hi2, lo, tw, lane, rev)
    return tuple(
        call(
            unpack_kernel,
            (S_((2048, 256), F32), S_((2048, 256), BF16), S_((2048, 256), F32)),
            (conv, corr, grad_out, gate, pre_gate, skip.reshape(1, 256)),
        )
    )


def solution(mesh):
    rows = P("ctx", "chan")
    return jax.shard_map(
        on_device,
        mesh=mesh,
        in_specs=(rows, rows, rows, rows, P(None, "ctx", "chan"), P("chan")),
        out_specs=(rows, rows, rows),
        check_vma=False,
    )
```

```python
import math

import numpy as np
import jax
import jax.numpy as jnp
import ml_dtypes
from jax import lax
from jax.experimental import pallas as pl
from jax.experimental.pallas import tpu as pltpu
from jax.sharding import PartitionSpec as P

F32 = jnp.float32
BF16 = jnp.bfloat16
N = 32768


def split_np(a):
    hi = a.astype(ml_dtypes.bfloat16)
    lo = (a - hi.astype(np.float64)).astype(ml_dtypes.bfloat16)
    return hi, lo


def tables():
    s = np.arange(256)
    ang = 2 * np.pi * ((s[:, None] * s[None, :]) % 256) / 256
    hi, lo = split_np(np.concatenate([np.cos(ang), np.sin(ang)], 0))
    kap = np.arange(9)[:, None] + 16 * np.arange(4)[None, :]
    both = np.stack([kap, kap + 64], 1)
    ang = 2 * np.pi * ((both[:, :, None, :] * s[None, None, :, None]) % N) / N
    ang = np.repeat(ang.reshape(9, 512, 4), 32, 2)
    twiddle = np.concatenate([np.cos(ang), np.sin(ang)], 2).astype(np.float32)
    r = np.repeat(np.arange(4), 32)
    ang = 2 * np.pi * np.arange(9)[:, None] * r[None, :] / 64
    half = 2 * np.pi * np.repeat(kap, 32, 1) / 128
    lane = np.stack([np.cos(ang), np.sin(ang), np.cos(half), np.sin(half)], 1)
    lane = np.concatenate([lane, lane], 1).astype(np.float32)
    rr = np.arange(4)
    c = np.kron(np.round(np.cos(np.pi * rr[:, None] * rr[None, :] / 2)), np.eye(32))
    n = np.kron(np.round(np.sin(np.pi * rr[:, None] * rr[None, :] / 2)), np.eye(32))
    fwd = np.block([[c, -n], [n, c]])
    inv = np.block([[c, n], [-n, c]])
    cross = np.stack([np.concatenate([fwd, fwd], 0), np.concatenate([inv, inv], 0)], 0)
    swap = np.eye(512).reshape(4, 4, 32, 512).transpose(1, 0, 2, 3).reshape(512, 512)
    rev = np.eye(64)[::-1]
    cross, swap, rev = (a.astype(ml_dtypes.bfloat16) for a in (cross, swap, rev))
    return np.concatenate([hi, hi], 1), lo, twiddle, lane, cross, swap, rev


C = [math.cos(2 * math.pi * q / 16) for q in range(16)]
S = [math.sin(2 * math.pi * q / 16) for q in range(16)]


def dft16_half(x):
    y = [None] * 9
    e = [x[i] + x[i + 4] for i in range(4)]
    f = [x[i] - x[i + 4] for i in range(4)]
    a, b = e[0] + e[2], e[1] + e[3]
    y[0] = (a + b, None)
    y[8] = (a - b, None)
    y[4] = (e[0] - e[2], e[3] - e[1])
    g, h = C[2] * (f[1] - f[3]), C[2] * (f[1] + f[3])
    y[2] = (f[0] + g, -(f[2] + h))
    y[6] = (f[0] - g, f[2] - h)
    d = [None] + [x[i] - x[8 - i] for i in (1, 2, 3)]
    s = [None] + [x[i] + x[8 - i] for i in (1, 2, 3)]
    for k in (1, 3):
        p = x[0] + d[2] * C[2 * k % 16]
        q = d[1] * C[k] + d[3] * C[3 * k % 16]
        u = s[1] * S[k] + s[3] * S[3 * k % 16]
        v = s[2] * S[2 * k % 16] + x[4] * S[4 * k % 16]
        y[k] = (p + q, -(u + v))
        y[8 - k] = (p - q, v - u)
    return y


def idft16_half(z):
    a, b = z[0][0] + z[8][0], z[0][0] - z[8][0]
    r4, i4 = z[4]
    e = [a + r4, b - i4, a - r4, b + i4]
    (r2, i2), (r6, i6) = z[2], z[6]
    m, n = r2 - r6, i2 + i6
    f = [r2 + r6, C[2] * (m - n), i6 - i2, -C[2] * (m + n)]
    out = [e[i] + f[i] for i in range(4)] + [e[i] - f[i] for i in range(4)]
    u = [0.0] * 5
    v = [0.0] * 5
    for k in (1, 3):
        rp, rm = z[k][0] + z[8 - k][0], z[k][0] - z[8 - k][0]
        ip, im = z[k][1] + z[8 - k][1], z[k][1] - z[8 - k][1]
        u[0] = u[0] + rp
        v[4] = v[4] + im * S[4 * k % 16]
        for q in (1, 2, 3):
            odd = q % 2 == 1
            u[q] = u[q] + (rm if odd else rp) * C[q * k % 16]
            v[q] = v[q] + (ip if odd else im) * S[q * k % 16]
    out[0] = out[0] + u[0]
    out[4] = out[4] - v[4]
    for q in (1, 2, 3):
        out[q] = out[q] + u[q] - v[q]
        out[8 - q] = out[8 - q] - u[q] - v[q]
    return out


TILE = 16


def split(value):
    high = value.astype(BF16)
    return high, (value - high.astype(F32)).astype(BF16)


def forward_q(x_ref, a_ref, lane_ref):
    def step(i, _):
        rows = pl.ds(pl.multiple_of(i * TILE, TILE), TILE)
        y = dft16_half([x_ref[q, rows, :].astype(F32) for q in range(8)])
        for k in range(9):
            re, im = y[k]
            lc, ls = lane_ref[k, 0:1, :], lane_ref[k, 1:2, :]
            if k == 0:
                im = jnp.zeros_like(re)
            elif im is None:
                re, im = re * lc, -(re * ls)
            else:
                re, im = re * lc + im * ls, im * lc - re * ls
            for part, at in ((re, 0), (im, 128)):
                high, low = split(part)
                a_ref[k, rows, at : at + 128] = high
                a_ref[k, rows, at + 256 : at + 384] = low
        return 0

    lax.fori_loop(0, 512 // TILE, step, 0)


def inverse_q(z_ref, emit, edge, scale):
    def step(i, _):
        row = pl.multiple_of(i * TILE, TILE)
        z = []
        for k in range(9):
            re = z_ref[pl.ds(1024 * k + row, TILE), :]
            im = z_ref[pl.ds(1024 * k + 512 + row, TILE), :]
            if k in (0, 8) and edge != 1.0:
                re = re * edge
            z.append((re, im))
        for q, value in enumerate(idft16_half(z)):
            emit(pl.ds(row, TILE), q, value * scale)
        return 0

    lax.fori_loop(0, 512 // TILE, step, 0)


def long_dot(hi_ref, lo_ref, g_ref):
    out = jnp.dot(hi_ref[...], g_ref[...], preferred_element_type=F32)
    out = out + jnp.dot(lo_ref[...], g_ref[0:256, :], preferred_element_type=F32)
    return out[0:256], out[256:512]


def forward_k(a_ref, k, tabs, g_ref):
    hi_ref, lo_ref, tw_ref, lane_ref, cross_ref = tabs
    d = jnp.dot(a_ref[k], cross_ref[0], preferred_element_type=F32)
    r0, i0 = d[0:256, 0:128], d[0:256, 128:256]
    r1, i1 = d[256:512, 0:128], d[256:512, 128:256]
    c, s = lane_ref[k, 2:3, :], lane_ref[k, 3:4, :]
    r1, i1 = r1 * c + i1 * s, i1 * c - r1 * s
    out = []
    for kh, (re, im) in enumerate(((r0 + r1, i0 + i1), (r0 - r1, i0 - i1))):
        c, s = tw_ref[k, 256 * kh : 256 * kh + 256, 0:128], tw_ref[k, 256 * kh : 256 * kh + 256, 128:256]
        re, im = re * c + im * s, im * c - re * s
        put(g_ref.at[kh], slice(0, 256), slice(256, 512), re, im)
        c, s = long_dot(hi_ref, lo_ref, g_ref.at[kh])
        out.append((c[:, 0:128] + s[:, 128:256], c[:, 128:256] - s[:, 0:128]))
    return out


def put(ref, rows, low_rows, re, im):
    for part, at in ((re, 0), (im, 128)):
        high, low = split(part)
        ref[rows, at : at + 128] = high
        ref[low_rows, at : at + 128] = low


def inverse_k(g_ref, k, tabs, a_ref, z_ref):
    hi_ref, lo_ref, tw_ref, lane_ref, cross_ref = tabs
    b = []
    for kh in range(2):
        c, s = long_dot(hi_ref, lo_ref, g_ref.at[kh])
        re, im = c[:, 0:128] - s[:, 128:256], c[:, 128:256] + s[:, 0:128]
        c, s = tw_ref[k, 256 * kh : 256 * kh + 256, 0:128], tw_ref[k, 256 * kh : 256 * kh + 256, 128:256]
        b.append((re * c - im * s, im * c + re * s))
    (r0, i0), (r1, i1) = b
    c, s = lane_ref[k, 2:3, :], lane_ref[k, 3:4, :]
    r1, i1, r0, i0 = r0 - r1, i0 - i1, r0 + r1, i0 + i1
    r1, i1 = r1 * c - i1 * s, i1 * c + r1 * s
    for at, (re, im) in ((0, (r0, i0)), (256, (r1, i1))):
        for part, lanes in ((re, 0), (im, 128)):
            high, low = split(part)
            a_ref[at : at + 256, lanes : lanes + 128] = high
            a_ref[at : at + 256, lanes + 256 : lanes + 384] = low
    d = jnp.dot(a_ref[...], cross_ref[1], preferred_element_type=F32)
    re, im = d[:, 0:128], d[:, 128:256]
    c, s = lane_ref[k, 0:1, :], lane_ref[k, 1:2, :]
    z_ref[pl.ds(1024 * k, 512), :] = re * c - im * s
    z_ref[pl.ds(1024 * k + 512, 512), :] = im * c + re * s


def exchange_groups(blocks, swap_ref):
    return jnp.dot(jnp.concatenate(blocks, 1), swap_ref[...], preferred_element_type=F32)


def unpack_kernel(conv_ref, corr_ref, grad_ref, gate_ref, pre_ref, skip_ref, swap_ref, in_ref, gg_ref, fg_ref):
    for half in range(2):
        lanes = slice(128 * half, 128 * half + 128)
        conv = exchange_groups([conv_ref[4 * half + e] for e in range(4)], swap_ref)
        corr = exchange_groups([corr_ref[4 * half + e] for e in range(4)], swap_ref)
        skip = skip_ref[:, lanes]
        for r in range(4):
            g = grad_ref[r, :, lanes].astype(F32)
            in_ref[r, :, lanes] = conv[:, 128 * r : 128 * r + 128] + skip * (g * gate_ref[r, :, lanes].astype(F32))
            gg_ref[r, :, lanes] = (g * pre_ref[r, :, lanes].astype(F32)).astype(BF16)
            fg_ref[r, :, lanes] = corr[:, 128 * r : 128 * r + 128]


MESH = pl.DeviceIdType.MESH
OFFSETS = ((2, 1), (2, 0), (1, 1), (3, 1), (1, 0), (3, 0), (0, 1))
SPEC = 9 * 1024
PACK = 256


def pack_dy(grad_ref, gate_ref, swap_ref, out_ref):
    def step(i, _):
        row = pl.multiple_of(i * PACK, PACK)
        for half in range(2):
            lanes = slice(128 * half, 128 * half + 128)
            at = [pl.ds(512 * r + row, PACK) for r in range(4)]
            dy = [(grad_ref[a, lanes].astype(F32) * gate_ref[a, lanes].astype(F32)).astype(BF16) for a in at]
            dy = exchange_groups(dy, swap_ref).astype(BF16)
            for e in range(4):
                out_ref[4 * half + e, pl.ds(row, PACK), :] = dy[:, 128 * e : 128 * e + 128]
        return 0

    lax.fori_loop(0, 512 // PACK, step, 0)


def pack_values(val_ref, swap_ref, out_ref):
    def step(i, _):
        row = pl.multiple_of(i * PACK, PACK)
        for half in range(2):
            lanes = slice(128 * half, 128 * half + 128)
            va = exchange_groups([val_ref[pl.ds(512 * r + row, PACK), lanes] for r in range(4)], swap_ref).astype(BF16)
            for e in range(4):
                out_ref[4 * half + e, pl.ds(row, PACK), :] = va[:, 128 * e : 128 * e + 128]
        return 0

    lax.fori_loop(0, 512 // PACK, step, 0)


def pack_rows(h_ref, swap_ref, rev_ref, out_ref, kq, slot, mirrored):
    parts = []
    for ri in range(2):
        for half in range(2):
            base = (2 * ri + half) * 4096 + kq
            blocks = []
            for kr in (3, 2, 1, 0) if mirrored else range(4):
                rows = [h_ref[pl.ds(base + 16 * kr + 64 * kh, 32, stride=128), :] for kh in range(2)]
                blocks.append(jnp.concatenate(rows, 0).astype(BF16))
            parts.append(jnp.concatenate(blocks, 1))
    wide = jnp.dot(jnp.concatenate(parts, 0), swap_ref[...], preferred_element_type=F32).astype(BF16)
    for n in range(4):
        rows = wide[64 * n : 64 * n + 64]
        if mirrored:
            rows = jnp.dot(rev_ref[...], rows, preferred_element_type=F32).astype(BF16)
        for e in range(4):
            out_ref[4 * (n % 2) + e, slot, n // 2] = rows[:, 128 * e : 128 * e + 128]


def pack_spectrum(h_ref, swap_ref, rev_ref, out_ref, chunk):
    if chunk == 0:
        pack_rows(h_ref, swap_ref, rev_ref, out_ref, 0, 0, False)
        pack_rows(h_ref, swap_ref, rev_ref, out_ref, 8, 1, False)
        pack_rows(h_ref, swap_ref, rev_ref, out_ref, 1, 2, False)
        pack_rows(h_ref, swap_ref, rev_ref, out_ref, 15, 3, True)
        return

    def step(i, _):
        k = 2 * chunk + i
        pack_rows(h_ref, swap_ref, rev_ref, out_ref, k, 4 * chunk + 2 * i, False)
        pack_rows(h_ref, swap_ref, rev_ref, out_ref, 16 - k, 4 * chunk + 2 * i + 1, True)
        return 0

    lax.fori_loop(0, 2, step, 0)


def conv_block(big_ref, h_ref, tabs, g_ref, a_ref, k, slot, mirror):
    for kh in range(2):
        for p in range(8):
            at = slice(32 * kh, 32 * kh + 32)
            hr = h_ref[p, slot, 0, at, :].astype(F32)
            hi = h_ref[p, slot, 1, at, :].astype(F32)
            if mirror is not None:
                hr = hr + h_ref[7 - p, mirror, 0, at, :].astype(F32)
                hi = hi - h_ref[7 - p, mirror, 1, at, :].astype(F32)
            first = SPEC + 1024 * k + 256 * kh + 32 * p
            dr, di = big_ref[pl.ds(first, 32), :], big_ref[pl.ds(first + 512, 32), :]
            rows, low = slice(32 * p, 32 * p + 32), slice(256 + 32 * p, 288 + 32 * p)
            put(g_ref.at[kh], rows, low, hr * dr + hi * di, hr * di - hi * dr)
    inverse_k(g_ref, k, tabs, a_ref, big_ref)


def main_kernel(
    grad_hbm, gate_hbm, val_hbm, h_hbm, hi_hbm, lo_hbm, tw_hbm, cross_hbm, swap_hbm, lane_ref, rev_ref,
    corr_out, conv_out,
    grad_v, gate_v, val_v, hi_v, lo_v, tw_v, cross_v, swap_v, tok_send, tok_recv, h_send, h_recv,
    big, dy_a, val_a, inv_a, dy_g, val_g, inv_g, res_send, load_sems, own_sems, send_sems, recv_sems,
):
    me = lax.axis_index("ctx")
    x, z = me // 2, me % 2
    peers = [((x + dx) % 4) * 2 + (z + dz) % 2 for dx, dz in OFFSETS]

    loads = [(grad_hbm, grad_v), (gate_hbm, gate_v), (swap_hbm, swap_v), (val_hbm, val_v)]
    for ri in range(2):
        for half in range(2):
            loads.append((h_hbm.at[ri, :, pl.ds(128 * half, 128)], big.at[pl.ds((2 * ri + half) * 4096, 4096), :]))
    loads += [(tw_hbm, tw_v), (hi_hbm, hi_v), (lo_hbm, lo_v), (cross_hbm, cross_v)]
    loads = [pltpu.make_async_copy(a, b, load_sems.at[i]) for i, (a, b) in enumerate(loads)]
    for c in loads:
        c.start()
    barrier = pltpu.get_barrier_semaphore()
    for peer in peers:
        pl.semaphore_signal(barrier, inc=1, device_id={"ctx": peer}, device_id_type=MESH)

    def exchange(group, source, target):
        copies = []
        for i, peer in enumerate(peers):
            c = pltpu.make_async_remote_copy(
                src_ref=source(peer), dst_ref=target,
                send_sem=send_sems.at[group, i], recv_sem=recv_sems.at[group, i],
                device_id={"ctx": peer}, device_id_type=MESH,
            )
            c.start()
            copies.append(c)
        own = pltpu.make_async_copy(source(me), target, own_sems.at[group])
        own.start()
        return copies, own

    def arrived(pair):
        for c in pair[0]:
            c.wait_recv()
        pair[1].wait()

    loads[0].wait()
    loads[1].wait()
    loads[2].wait()
    pack_dy(grad_v, gate_v, swap_v, tok_send.at[0])
    pl.semaphore_wait(barrier, 7)
    dy_move = exchange(0, lambda d: tok_send.at[0, d], tok_recv.at[0, me])
    loads[3].wait()
    pack_values(val_v, swap_v, tok_send.at[1])
    val_move = exchange(1, lambda d: tok_send.at[1, d], tok_recv.at[1, me])
    for c in loads[4:8]:
        c.wait()
    h_moves = []
    for chunk in range(4):
        pack_spectrum(big, swap_v, rev_ref, h_send, chunk)
        part = pl.ds(4 * chunk, 4)
        h_moves.append(exchange(2 + chunk, lambda d: h_send.at[d, part], h_recv.at[me, part]))
    for c in loads[8:]:
        c.wait()

    tabs = (hi_v, lo_v, tw_v, lane_ref, cross_v)
    arrived(dy_move)
    forward_q(tok_recv.at[0], dy_a, lane_ref)
    arrived(val_move)
    forward_q(tok_recv.at[1], val_a, lane_ref)

    def block(k, _):
        dy_s = forward_k(dy_a, k, tabs, dy_g)
        val_s = forward_k(val_a, k, tabs, val_g)
        for kh in range(2):
            (dr, di), (vr, vi) = dy_s[kh], val_s[kh]
            first = SPEC + 1024 * k + 256 * kh
            big[pl.ds(first, 256), :] = dr
            big[pl.ds(first + 512, 256), :] = di
            put(inv_g.at[kh], slice(0, 256), slice(256, 512), vr * dr + vi * di, vr * di - vi * dr)
        inverse_k(inv_g, k, tabs, inv_a, big)
        return 0

    lax.fori_loop(0, 9, block, 0)

    def emit_to(n):
        def emit(rows, q, value):
            res_send[n, q, rows, :] = value.astype(BF16)
        return emit

    inverse_q(big, emit_to(0), 0.5, 2.0 / N)
    corr_move = exchange(6, lambda d: res_send.at[0, d], corr_out.at[me])

    for chunk in range(4):
        arrived(h_moves[chunk])
        if chunk == 0:
            conv_block(big, h_recv, tabs, inv_g, inv_a, 0, 0, None)
            conv_block(big, h_recv, tabs, inv_g, inv_a, 8, 1, None)
            conv_block(big, h_recv, tabs, inv_g, inv_a, 1, 2, 3)
        else:
            def step(i, _, chunk=chunk):
                slot = 4 * chunk + 2 * i
                conv_block(big, h_recv, tabs, inv_g, inv_a, 2 * chunk + i, slot, slot + 1)
                return 0
            lax.fori_loop(0, 2, step, 0)
    inverse_q(big, emit_to(1), 1.0, 1.0 / N)
    conv_move = exchange(7, lambda d: res_send.at[1, d], conv_out.at[me])
    arrived(corr_move)
    arrived(conv_move)
    for pair in (dy_move, val_move, *h_moves, corr_move, conv_move):
        for c in pair[0]:
            c.wait_send()


def on_device(grad_out, values, gate, pre_gate, filter_spectrum, skip):
    S_ = jax.ShapeDtypeStruct
    hi, lo, tw, lane, cross, swap, rev = (jnp.asarray(a) for a in tables())
    anywhere = pl.BlockSpec(memory_space=pl.ANY)
    vmem = pl.BlockSpec(memory_space=pltpu.VMEM)
    result = S_((8, 512, 128), BF16)
    tokens = pltpu.VMEM((2048, 256), BF16)
    corr, conv = pl.pallas_call(
        main_kernel,
        out_shape=(result, result),
        in_specs=[anywhere] * 9 + [vmem] * 2,
        out_specs=(anywhere, anywhere),
        scratch_shapes=[
            tokens,
            tokens,
            tokens,
            pltpu.VMEM((512, 512), BF16),
            pltpu.VMEM((512, 256), BF16),
            pltpu.VMEM((9, 512, 256), F32),
            pltpu.VMEM((2, 512, 256), BF16),
            pltpu.VMEM((512, 512), BF16),
            pltpu.VMEM((2, 8, 512, 128), BF16),
            pltpu.VMEM((2, 8, 512, 128), BF16),
            pltpu.VMEM((8, 16, 2, 64, 128), BF16),
            pltpu.VMEM((8, 16, 2, 64, 128), BF16),
            pltpu.VMEM((18 * 1024, 128), F32),
            pltpu.VMEM((9, 512, 512), BF16),
            pltpu.VMEM((9, 512, 512), BF16),
            pltpu.VMEM((512, 512), BF16),
            pltpu.VMEM((2, 512, 256), BF16),
            pltpu.VMEM((2, 512, 256), BF16),
            pltpu.VMEM((2, 512, 256), BF16),
            pltpu.VMEM((2, 8, 512, 128), BF16),
            pltpu.SemaphoreType.DMA((12,)),
            pltpu.SemaphoreType.DMA((8,)),
            pltpu.SemaphoreType.DMA((8, 7)),
            pltpu.SemaphoreType.DMA((8, 7)),
        ],
        compiler_params=pltpu.CompilerParams(collective_id=0, has_side_effects=True, vmem_limit_bytes=58 << 20),
    )(grad_out, gate, values, filter_spectrum, hi, lo, tw, cross, swap, lane, rev)

    rows = 128
    packed = pl.BlockSpec((8, rows, 128), lambda i: (0, i, 0))
    plain = pl.BlockSpec((4, rows, 256), lambda i: (0, i, 0))
    whole = lambda shape: pl.BlockSpec(shape, lambda i: (0, 0))
    fold = lambda a: a.reshape(4, 512, 256)
    outs = pl.pallas_call(
        unpack_kernel,
        grid=(512 // rows,),
        out_shape=(S_((4, 512, 256), F32), S_((4, 512, 256), BF16), S_((4, 512, 256), F32)),
        in_specs=[packed, packed, plain, plain, plain, whole((1, 256)), whole((512, 512))],
        out_specs=(plain, plain, plain),
        compiler_params=pltpu.CompilerParams(vmem_limit_bytes=32 << 20),
    )(conv, corr, fold(grad_out), fold(gate), fold(pre_gate), skip.reshape(1, 256), swap)
    return tuple(a.reshape(2048, 256) for a in outs)


def solution(mesh):
    rows = P("ctx", "chan")
    return jax.shard_map(
        on_device,
        mesh=mesh,
        in_specs=(rows, rows, rows, rows, P(None, "ctx", "chan"), P("chan")),
        out_specs=(rows, rows, rows),
        check_vma=False,
    )
```

```python
import math

import numpy as np
import jax
import jax.numpy as jnp
import ml_dtypes
from jax import lax
from jax.experimental import pallas as pl
from jax.experimental.pallas import tpu as pltpu
from jax.sharding import PartitionSpec as P

F32 = jnp.float32
BF16 = jnp.bfloat16
N = 32768


def split_np(a):
    hi = a.astype(ml_dtypes.bfloat16)
    lo = (a - hi.astype(np.float64)).astype(ml_dtypes.bfloat16)
    return hi, lo


def tables():
    s = np.arange(256)
    ang = 2 * np.pi * ((s[:, None] * s[None, :]) % 256) / 256
    hi, lo = split_np(np.concatenate([np.cos(ang), np.sin(ang)], 0))
    kap = np.arange(9)[:, None] + 16 * np.arange(4)[None, :]
    both = np.stack([kap, kap + 64], 1)
    ang = 2 * np.pi * ((both[:, :, None, :] * s[None, None, :, None]) % N) / N
    ang = np.repeat(ang.reshape(9, 512, 4), 32, 2)
    twiddle = np.concatenate([np.cos(ang), np.sin(ang)], 2).astype(np.float32)
    r = np.repeat(np.arange(4), 32)
    ang = 2 * np.pi * np.arange(9)[:, None] * r[None, :] / 64
    half = 2 * np.pi * np.repeat(kap, 32, 1) / 128
    lane = np.stack([np.cos(ang), np.sin(ang), np.cos(half), np.sin(half)], 1)
    lane = np.concatenate([lane, lane], 1).astype(np.float32)
    rr = np.arange(4)
    c = np.kron(np.round(np.cos(np.pi * rr[:, None] * rr[None, :] / 2)), np.eye(32))
    n = np.kron(np.round(np.sin(np.pi * rr[:, None] * rr[None, :] / 2)), np.eye(32))
    fwd = np.block([[c, -n], [n, c]])
    inv = np.block([[c, n], [-n, c]])
    cross = np.stack([np.concatenate([fwd, fwd], 0), np.concatenate([inv, inv], 0)], 0)
    swap = np.eye(512).reshape(4, 4, 32, 512).transpose(1, 0, 2, 3).reshape(512, 512)
    rev = np.eye(64)[::-1]
    cross, swap, rev = (a.astype(ml_dtypes.bfloat16) for a in (cross, swap, rev))
    return np.concatenate([hi, hi], 1), lo, twiddle, lane, cross, swap, rev


C = [math.cos(2 * math.pi * q / 16) for q in range(16)]
S = [math.sin(2 * math.pi * q / 16) for q in range(16)]


def dft16_half(x):
    y = [None] * 9
    e = [x[i] + x[i + 4] for i in range(4)]
    f = [x[i] - x[i + 4] for i in range(4)]
    a, b = e[0] + e[2], e[1] + e[3]
    y[0] = (a + b, None)
    y[8] = (a - b, None)
    y[4] = (e[0] - e[2], e[3] - e[1])
    g, h = C[2] * (f[1] - f[3]), C[2] * (f[1] + f[3])
    y[2] = (f[0] + g, -(f[2] + h))
    y[6] = (f[0] - g, f[2] - h)
    d = [None] + [x[i] - x[8 - i] for i in (1, 2, 3)]
    s = [None] + [x[i] + x[8 - i] for i in (1, 2, 3)]
    for k in (1, 3):
        p = x[0] + d[2] * C[2 * k % 16]
        q = d[1] * C[k] + d[3] * C[3 * k % 16]
        u = s[1] * S[k] + s[3] * S[3 * k % 16]
        v = s[2] * S[2 * k % 16] + x[4] * S[4 * k % 16]
        y[k] = (p + q, -(u + v))
        y[8 - k] = (p - q, v - u)
    return y


def idft16_half(z):
    a, b = z[0][0] + z[8][0], z[0][0] - z[8][0]
    r4, i4 = z[4]
    e = [a + r4, b - i4, a - r4, b + i4]
    (r2, i2), (r6, i6) = z[2], z[6]
    m, n = r2 - r6, i2 + i6
    f = [r2 + r6, C[2] * (m - n), i6 - i2, -C[2] * (m + n)]
    out = [e[i] + f[i] for i in range(4)] + [e[i] - f[i] for i in range(4)]
    u = [0.0] * 5
    v = [0.0] * 5
    for k in (1, 3):
        rp, rm = z[k][0] + z[8 - k][0], z[k][0] - z[8 - k][0]
        ip, im = z[k][1] + z[8 - k][1], z[k][1] - z[8 - k][1]
        u[0] = u[0] + rp
        v[4] = v[4] + im * S[4 * k % 16]
        for q in (1, 2, 3):
            odd = q % 2 == 1
            u[q] = u[q] + (rm if odd else rp) * C[q * k % 16]
            v[q] = v[q] + (ip if odd else im) * S[q * k % 16]
    out[0] = out[0] + u[0]
    out[4] = out[4] - v[4]
    for q in (1, 2, 3):
        out[q] = out[q] + u[q] - v[q]
        out[8 - q] = out[8 - q] - u[q] - v[q]
    return out


TILE = 16


def split(value):
    high = value.astype(BF16)
    return high, (value - high.astype(F32)).astype(BF16)


def forward_q(x_ref, a_ref, lane_ref, part):
    def step(i, _):
        rows = pl.ds(pl.multiple_of(i * TILE, TILE), TILE)
        y = dft16_half([x_ref[q, rows, :].astype(F32) for q in range(8)])
        for k in range(9):
            re, im = y[k]
            lc, ls = lane_ref[k, 0:1, :], lane_ref[k, 1:2, :]
            if k == 0:
                im = jnp.zeros_like(re)
            elif im is None:
                re, im = re * lc, -(re * ls)
            else:
                re, im = re * lc + im * ls, im * lc - re * ls
            for part, at in ((re, 0), (im, 128)):
                high, low = split(part)
                a_ref[k, rows, at : at + 128] = high
                a_ref[k, rows, at + 256 : at + 384] = low
        return 0

    lax.fori_loop(part * (256 // TILE), (part + 1) * (256 // TILE), step, 0)


def inverse_q(z_ref, emit, edge, scale, part):
    def step(i, _):
        row = pl.multiple_of(i * TILE, TILE)
        z = []
        for k in range(9):
            re = z_ref[pl.ds(1024 * k + row, TILE), :]
            im = z_ref[pl.ds(1024 * k + 512 + row, TILE), :]
            if k in (0, 8) and edge != 1.0:
                re = re * edge
            z.append((re, im))
        for q, value in enumerate(idft16_half(z)):
            emit(pl.ds(row, TILE), q, value * scale)
        return 0

    lax.fori_loop(part * (256 // TILE), (part + 1) * (256 // TILE), step, 0)


def long_dot(hi_ref, lo_ref, g_ref):
    out = jnp.dot(hi_ref[...], g_ref[...], preferred_element_type=F32)
    out = out + jnp.dot(lo_ref[...], g_ref[0:256, :], preferred_element_type=F32)
    return out[0:256], out[256:512]


def forward_k(a_ref, k, tabs, g_ref):
    hi_ref, lo_ref, tw_ref, lane_ref, cross_ref = tabs
    d = jnp.dot(a_ref[k], cross_ref[0], preferred_element_type=F32)
    r0, i0 = d[0:256, 0:128], d[0:256, 128:256]
    r1, i1 = d[256:512, 0:128], d[256:512, 128:256]
    c, s = lane_ref[k, 2:3, :], lane_ref[k, 3:4, :]
    r1, i1 = r1 * c + i1 * s, i1 * c - r1 * s
    out = []
    for kh, (re, im) in enumerate(((r0 + r1, i0 + i1), (r0 - r1, i0 - i1))):
        c, s = tw_ref[k, 256 * kh : 256 * kh + 256, 0:128], tw_ref[k, 256 * kh : 256 * kh + 256, 128:256]
        re, im = re * c + im * s, im * c - re * s
        put(g_ref.at[kh], slice(0, 256), slice(256, 512), re, im)
        c, s = long_dot(hi_ref, lo_ref, g_ref.at[kh])
        out.append((c[:, 0:128] + s[:, 128:256], c[:, 128:256] - s[:, 0:128]))
    return out


def put(ref, rows, low_rows, re, im):
    for part, at in ((re, 0), (im, 128)):
        high, low = split(part)
        ref[rows, at : at + 128] = high
        ref[low_rows, at : at + 128] = low


def inverse_k(g_ref, k, tabs, a_ref, z_ref):
    hi_ref, lo_ref, tw_ref, lane_ref, cross_ref = tabs
    b = []
    for kh in range(2):
        c, s = long_dot(hi_ref, lo_ref, g_ref.at[kh])
        re, im = c[:, 0:128] - s[:, 128:256], c[:, 128:256] + s[:, 0:128]
        c, s = tw_ref[k, 256 * kh : 256 * kh + 256, 0:128], tw_ref[k, 256 * kh : 256 * kh + 256, 128:256]
        b.append((re * c - im * s, im * c + re * s))
    (r0, i0), (r1, i1) = b
    c, s = lane_ref[k, 2:3, :], lane_ref[k, 3:4, :]
    r1, i1, r0, i0 = r0 - r1, i0 - i1, r0 + r1, i0 + i1
    r1, i1 = r1 * c - i1 * s, i1 * c + r1 * s
    for at, (re, im) in ((0, (r0, i0)), (256, (r1, i1))):
        for part, lanes in ((re, 0), (im, 128)):
            high, low = split(part)
            a_ref[at : at + 256, lanes : lanes + 128] = high
            a_ref[at : at + 256, lanes + 256 : lanes + 384] = low
    d = jnp.dot(a_ref[...], cross_ref[1], preferred_element_type=F32)
    re, im = d[:, 0:128], d[:, 128:256]
    c, s = lane_ref[k, 0:1, :], lane_ref[k, 1:2, :]
    z_ref[pl.ds(1024 * k, 512), :] = re * c - im * s
    z_ref[pl.ds(1024 * k + 512, 512), :] = im * c + re * s


def exchange_groups(blocks, swap_ref):
    return jnp.dot(jnp.concatenate(blocks, 1), swap_ref[...], preferred_element_type=F32)


def unpack_kernel(conv_ref, corr_ref, grad_ref, gate_ref, pre_ref, skip_ref, swap_ref, in_ref, gg_ref, fg_ref):
    for half in range(2):
        lanes = slice(128 * half, 128 * half + 128)
        conv = exchange_groups([conv_ref[4 * half + e] for e in range(4)], swap_ref)
        corr = exchange_groups([corr_ref[4 * half + e] for e in range(4)], swap_ref)
        skip = skip_ref[:, lanes]
        for r in range(4):
            g = grad_ref[r, :, lanes].astype(F32)
            in_ref[r, :, lanes] = conv[:, 128 * r : 128 * r + 128] + skip * (g * gate_ref[r, :, lanes].astype(F32))
            gg_ref[r, :, lanes] = (g * pre_ref[r, :, lanes].astype(F32)).astype(BF16)
            fg_ref[r, :, lanes] = corr[:, 128 * r : 128 * r + 128]


MESH = pl.DeviceIdType.MESH
OFFSETS = ((2, 0), (0, 1), (2, 1), (1, 1), (3, 0), (3, 1), (1, 0))
CHUNKS = ((0, 4), (4, 4), (8, 4), (12, 2), (14, 2))
SPEC = 9 * 1024
PACK = 256
CORR_AFTER = 3


def pack_dy(grad_ref, gate_ref, swap_ref, out_ref, part):
    for half in range(2):
        lanes = slice(128 * half, 128 * half + 128)
        at = [slice(512 * r + PACK * part, 512 * r + PACK * part + PACK) for r in range(4)]
        dy = [(grad_ref[a, lanes].astype(F32) * gate_ref[a, lanes].astype(F32)).astype(BF16) for a in at]
        dy = exchange_groups(dy, swap_ref).astype(BF16)
        for e in range(4):
            out_ref[4 * half + e, PACK * part : PACK * part + PACK, :] = dy[:, 128 * e : 128 * e + 128]


def pack_values(val_ref, swap_ref, out_ref, part):
    for half in range(2):
        lanes = slice(128 * half, 128 * half + 128)
        at = [slice(512 * r + PACK * part, 512 * r + PACK * part + PACK) for r in range(4)]
        va = exchange_groups([val_ref[a, lanes] for a in at], swap_ref).astype(BF16)
        for e in range(4):
            out_ref[4 * half + e, PACK * part : PACK * part + PACK, :] = va[:, 128 * e : 128 * e + 128]


def pack_rows(h_ref, swap_ref, rev_ref, out_ref, kq, slot, mirrored):
    parts = []
    for ri in range(2):
        for half in range(2):
            base = (2 * ri + half) * 4096 + kq
            blocks = []
            for kr in (3, 2, 1, 0) if mirrored else range(4):
                rows = [h_ref[pl.ds(base + 16 * kr + 64 * kh, 32, stride=128), :] for kh in range(2)]
                blocks.append(jnp.concatenate(rows, 0).astype(BF16))
            parts.append(jnp.concatenate(blocks, 1))
    wide = jnp.dot(jnp.concatenate(parts, 0), swap_ref[...], preferred_element_type=F32).astype(BF16)
    for n in range(4):
        rows = wide[64 * n : 64 * n + 64]
        if mirrored:
            rows = jnp.dot(rev_ref[...], rows, preferred_element_type=F32).astype(BF16)
        for e in range(4):
            out_ref[4 * (n % 2) + e, slot, n // 2] = rows[:, 128 * e : 128 * e + 128]


def pack_spectrum(h_ref, swap_ref, rev_ref, out_ref, chunk):
    first, count = CHUNKS[chunk]
    if first == 0:
        pack_rows(h_ref, swap_ref, rev_ref, out_ref, 0, 0, False)
        pack_rows(h_ref, swap_ref, rev_ref, out_ref, 8, 1, False)
        first, count = 2, count - 2

    def step(i, _):
        slot = first + 2 * i
        k = slot // 2
        pack_rows(h_ref, swap_ref, rev_ref, out_ref, k, slot, False)
        pack_rows(h_ref, swap_ref, rev_ref, out_ref, 16 - k, slot + 1, True)
        return 0

    lax.fori_loop(0, count // 2, step, 0)


def conv_block(big_ref, h_ref, tabs, g_ref, a_ref, k, slot, mirror):
    for kh in range(2):
        for p in range(8):
            at = slice(32 * kh, 32 * kh + 32)
            hr = h_ref[p, slot, 0, at, :].astype(F32)
            hi = h_ref[p, slot, 1, at, :].astype(F32)
            if mirror is not None:
                hr = hr + h_ref[7 - p, mirror, 0, at, :].astype(F32)
                hi = hi - h_ref[7 - p, mirror, 1, at, :].astype(F32)
            first = SPEC + 1024 * k + 256 * kh + 32 * p
            dr, di = big_ref[pl.ds(first, 32), :], big_ref[pl.ds(first + 512, 32), :]
            rows, low = slice(32 * p, 32 * p + 32), slice(256 + 32 * p, 288 + 32 * p)
            put(g_ref.at[kh], rows, low, hr * dr + hi * di, hr * di - hi * dr)
    inverse_k(g_ref, k, tabs, a_ref, big_ref)


def main_kernel(
    grad_hbm, gate_hbm, val_hbm, h_hbm, hi_hbm, lo_hbm, tw_hbm, cross_hbm, swap_hbm, lane_ref, rev_ref,
    corr_out, conv_out,
    grad_v, gate_v, val_v, hi_v, lo_v, tw_v, cross_v, swap_v, tok_send, tok_recv, h_send, h_recv,
    big, dy_a, val_a, inv_a, dy_g, val_g, inv_g, res_send, load_sems, own_sems, send_sems, recv_sems,
):
    me = lax.axis_index("ctx")
    x, z = me // 2, me % 2
    peers = [((x + dx) % 4) * 2 + (z + dz) % 2 for dx, dz in OFFSETS]

    loads = [(grad_hbm, grad_v), (gate_hbm, gate_v), (swap_hbm, swap_v), (val_hbm, val_v)]
    for ri in range(2):
        for half in range(2):
            loads.append((h_hbm.at[ri, :, pl.ds(128 * half, 128)], big.at[pl.ds((2 * ri + half) * 4096, 4096), :]))
    loads += [(tw_hbm, tw_v), (hi_hbm, hi_v), (lo_hbm, lo_v), (cross_hbm, cross_v)]
    loads = [pltpu.make_async_copy(a, b, load_sems.at[i]) for i, (a, b) in enumerate(loads)]
    for c in loads[:4]:
        c.start()
    barrier = pltpu.get_barrier_semaphore()
    for peer in peers:
        pl.semaphore_signal(barrier, inc=1, device_id={"ctx": peer}, device_id_type=MESH)

    def exchange(group, source, target):
        copies = []
        for i, peer in enumerate(peers):
            c = pltpu.make_async_remote_copy(
                src_ref=source(peer), dst_ref=target,
                send_sem=send_sems.at[group, i], recv_sem=recv_sems.at[group, i],
                device_id={"ctx": peer}, device_id_type=MESH,
            )
            c.start()
            copies.append(c)
        own = pltpu.make_async_copy(source(me), target, own_sems.at[group])
        own.start()
        return copies, own

    def arrived(pair):
        for c in pair[0]:
            c.wait_recv()
        pair[1].wait()

    halves = [pl.ds(256 * part, 256) for part in range(2)]
    for c in loads[:3]:
        c.wait()
    dy_moves, val_moves, h_moves = [], [], []
    for part in range(2):
        pack_dy(grad_v, gate_v, swap_v, tok_send.at[0], part)
        if part == 0:
            pl.semaphore_wait(barrier, 7)
        at = halves[part]
        dy_moves.append(exchange(part, lambda d: tok_send.at[0, d, at], tok_recv.at[0, me, at]))
    for c in loads[4:]:
        c.start()
    loads[3].wait()
    for part in range(2):
        pack_values(val_v, swap_v, tok_send.at[1], part)
        at = halves[part]
        val_moves.append(exchange(2 + part, lambda d: tok_send.at[1, d, at], tok_recv.at[1, me, at]))
    for c in loads[4:8]:
        c.wait()
    for chunk, (first, count) in enumerate(CHUNKS):
        pack_spectrum(big, swap_v, rev_ref, h_send, chunk)
        at = pl.ds(first, count)
        h_moves.append(exchange(4 + chunk, lambda d: h_send.at[d, at], h_recv.at[me, at]))
    for c in loads[8:]:
        c.wait()

    tabs = (hi_v, lo_v, tw_v, lane_ref, cross_v)
    for n, (moves, a_ref) in enumerate(((dy_moves, dy_a), (val_moves, val_a))):
        for part in range(2):
            arrived(moves[part])
            forward_q(tok_recv.at[n], a_ref, lane_ref, part)

    def block(k, _):
        dy_s = forward_k(dy_a, k, tabs, dy_g)
        val_s = forward_k(val_a, k, tabs, val_g)
        for kh in range(2):
            (dr, di), (vr, vi) = dy_s[kh], val_s[kh]
            first = SPEC + 1024 * k + 256 * kh
            big[pl.ds(first, 256), :] = dr
            big[pl.ds(first + 512, 256), :] = di
            put(inv_g.at[kh], slice(0, 256), slice(256, 512), vr * dr + vi * di, vr * di - vi * dr)
        inverse_k(inv_g, k, tabs, inv_a, big)
        return 0

    lax.fori_loop(0, 9, block, 0)

    def emit_to(n):
        def emit(rows, q, value):
            res_send[n, q, rows, :] = value.astype(BF16)
        return emit

    for part in range(2):
        inverse_q(big, emit_to(0), 0.5, 2.0 / N, part)

    conv_moves = []
    for chunk, (first, count) in enumerate(CHUNKS):
        arrived(h_moves[chunk])
        if chunk == CORR_AFTER:
            corr_move = exchange(9, lambda d: res_send.at[0, d], corr_out.at[me])
        if first == 0:
            conv_block(big, h_recv, tabs, inv_g, inv_a, 0, 0, None)
            conv_block(big, h_recv, tabs, inv_g, inv_a, 8, 1, None)
            first, count = 2, count - 2

        def step(i, _, first=first):
            slot = first + 2 * i
            conv_block(big, h_recv, tabs, inv_g, inv_a, slot // 2, slot, slot + 1)
            return 0

        lax.fori_loop(0, count // 2, step, 0)
    for part in range(2):
        inverse_q(big, emit_to(1), 1.0, 1.0 / N, part)
        at = halves[part]
        conv_moves.append(exchange(10 + part, lambda d: res_send.at[1, d, at], conv_out.at[me, at]))
    moves = (*dy_moves, *val_moves, *h_moves, corr_move, *conv_moves)
    for pair in (corr_move, *conv_moves):
        arrived(pair)
    for pair in moves:
        for c in pair[0]:
            c.wait_send()


def on_device(grad_out, values, gate, pre_gate, filter_spectrum, skip):
    S_ = jax.ShapeDtypeStruct
    hi, lo, tw, lane, cross, swap, rev = (jnp.asarray(a) for a in tables())
    anywhere = pl.BlockSpec(memory_space=pl.ANY)
    vmem = pl.BlockSpec(memory_space=pltpu.VMEM)
    result = pltpu.VMEM((8, 512, 128), BF16)
    tokens = pltpu.VMEM((2048, 256), BF16)
    corr, conv = pl.pallas_call(
        main_kernel,
        out_shape=(result, result),
        in_specs=[anywhere] * 9 + [vmem] * 2,
        out_specs=(anywhere, anywhere),
        scratch_shapes=[
            tokens,
            tokens,
            tokens,
            pltpu.VMEM((512, 512), BF16),
            pltpu.VMEM((512, 256), BF16),
            pltpu.VMEM((9, 512, 256), F32),
            pltpu.VMEM((2, 512, 256), BF16),
            pltpu.VMEM((512, 512), BF16),
            pltpu.VMEM((2, 8, 512, 128), BF16),
            pltpu.VMEM((2, 8, 512, 128), BF16),
            pltpu.VMEM((8, 16, 2, 64, 128), BF16),
            pltpu.VMEM((8, 16, 2, 64, 128), BF16),
            pltpu.VMEM((18 * 1024, 128), F32),
            pltpu.VMEM((9, 512, 512), BF16),
            pltpu.VMEM((9, 512, 512), BF16),
            pltpu.VMEM((512, 512), BF16),
            pltpu.VMEM((2, 512, 256), BF16),
            pltpu.VMEM((2, 512, 256), BF16),
            pltpu.VMEM((2, 512, 256), BF16),
            pltpu.VMEM((2, 8, 512, 128), BF16),
            pltpu.SemaphoreType.DMA((12,)),
            pltpu.SemaphoreType.DMA((12,)),
            pltpu.SemaphoreType.DMA((12, 7)),
            pltpu.SemaphoreType.DMA((12, 7)),
        ],
        compiler_params=pltpu.CompilerParams(collective_id=0, has_side_effects=True, vmem_limit_bytes=58 << 20),
    )(grad_out, gate, values, filter_spectrum, hi, lo, tw, cross, swap, lane, rev)

    rows = 128
    packed = pl.BlockSpec((8, rows, 128), lambda i: (0, i, 0))
    plain = pl.BlockSpec((4, rows, 256), lambda i: (0, i, 0))
    whole = lambda shape: pl.BlockSpec(shape, lambda i: (0, 0))
    fold = lambda a: a.reshape(4, 512, 256)
    outs = pl.pallas_call(
        unpack_kernel,
        grid=(512 // rows,),
        out_shape=(S_((4, 512, 256), F32), S_((4, 512, 256), BF16), S_((4, 512, 256), F32)),
        in_specs=[packed, packed, plain, plain, plain, whole((1, 256)), whole((512, 512))],
        out_specs=(plain, plain, plain),
        compiler_params=pltpu.CompilerParams(vmem_limit_bytes=32 << 20),
    )(conv, corr, fold(grad_out), fold(gate), fold(pre_gate), skip.reshape(1, 256), swap)
    return tuple(a.reshape(2048, 256) for a in outs)


def solution(mesh):
    rows = P("ctx", "chan")
    return jax.shard_map(
        on_device,
        mesh=mesh,
        in_specs=(rows, rows, rows, rows, P(None, "ctx", "chan"), P("chan")),
        out_specs=(rows, rows, rows),
        check_vma=False,
    )
```

```python
import math

import numpy as np
import jax
import jax.numpy as jnp
import ml_dtypes
from jax import lax
from jax.experimental import pallas as pl
from jax.experimental.pallas import tpu as pltpu
from jax.sharding import PartitionSpec as P

F32 = jnp.float32
BF16 = jnp.bfloat16
N = 32768


def split_np(a):
    hi = a.astype(ml_dtypes.bfloat16)
    lo = (a - hi.astype(np.float64)).astype(ml_dtypes.bfloat16)
    return hi, lo


def tables():
    s = np.arange(256)
    ang = 2 * np.pi * ((s[:, None] * s[None, :]) % 256) / 256
    hi, lo = split_np(np.concatenate([np.cos(ang), np.sin(ang)], 0))
    kap = np.arange(9)[:, None] + 16 * np.arange(4)[None, :]
    both = np.stack([kap, kap + 64], 1)
    ang = 2 * np.pi * ((both[:, :, None, :] * s[None, None, :, None]) % N) / N
    ang = np.repeat(ang.reshape(9, 512, 4), 32, 2)
    twiddle = np.concatenate([np.cos(ang), np.sin(ang)], 2).astype(np.float32)
    r = np.repeat(np.arange(4), 32)
    ang = 2 * np.pi * np.arange(9)[:, None] * r[None, :] / 64
    half = 2 * np.pi * np.repeat(kap, 32, 1) / 128
    lane = np.stack([np.cos(ang), np.sin(ang), np.cos(half), np.sin(half)], 1)
    lane = np.concatenate([lane, lane], 1).astype(np.float32)
    rr = np.arange(4)
    c = np.kron(np.round(np.cos(np.pi * rr[:, None] * rr[None, :] / 2)), np.eye(32))
    n = np.kron(np.round(np.sin(np.pi * rr[:, None] * rr[None, :] / 2)), np.eye(32))
    fwd = np.block([[c, -n], [n, c]])
    inv = np.block([[c, n], [-n, c]])
    cross = np.stack([np.concatenate([fwd, fwd], 0), np.concatenate([inv, inv], 0)], 0)
    swap = np.eye(512).reshape(4, 4, 32, 512).transpose(1, 0, 2, 3).reshape(512, 512)
    rev = np.eye(64)[::-1]
    cross, swap, rev = (a.astype(ml_dtypes.bfloat16) for a in (cross, swap, rev))
    return np.concatenate([hi, hi], 1), lo, twiddle, lane, cross, swap, rev


C = [math.cos(2 * math.pi * q / 16) for q in range(16)]
S = [math.sin(2 * math.pi * q / 16) for q in range(16)]


def dft16_half(x):
    y = [None] * 9
    e = [x[i] + x[i + 4] for i in range(4)]
    f = [x[i] - x[i + 4] for i in range(4)]
    a, b = e[0] + e[2], e[1] + e[3]
    y[0] = (a + b, None)
    y[8] = (a - b, None)
    y[4] = (e[0] - e[2], e[3] - e[1])
    g, h = C[2] * (f[1] - f[3]), C[2] * (f[1] + f[3])
    y[2] = (f[0] + g, -(f[2] + h))
    y[6] = (f[0] - g, f[2] - h)
    d = [None] + [x[i] - x[8 - i] for i in (1, 2, 3)]
    s = [None] + [x[i] + x[8 - i] for i in (1, 2, 3)]
    for k in (1, 3):
        p = x[0] + d[2] * C[2 * k % 16]
        q = d[1] * C[k] + d[3] * C[3 * k % 16]
        u = s[1] * S[k] + s[3] * S[3 * k % 16]
        v = s[2] * S[2 * k % 16] + x[4] * S[4 * k % 16]
        y[k] = (p + q, -(u + v))
        y[8 - k] = (p - q, v - u)
    return y


def idft16_half(z):
    a, b = z[0][0] + z[8][0], z[0][0] - z[8][0]
    r4, i4 = z[4]
    e = [a + r4, b - i4, a - r4, b + i4]
    (r2, i2), (r6, i6) = z[2], z[6]
    m, n = r2 - r6, i2 + i6
    f = [r2 + r6, C[2] * (m - n), i6 - i2, -C[2] * (m + n)]
    out = [e[i] + f[i] for i in range(4)] + [e[i] - f[i] for i in range(4)]
    u = [0.0] * 5
    v = [0.0] * 5
    for k in (1, 3):
        rp, rm = z[k][0] + z[8 - k][0], z[k][0] - z[8 - k][0]
        ip, im = z[k][1] + z[8 - k][1], z[k][1] - z[8 - k][1]
        u[0] = u[0] + rp
        v[4] = v[4] + im * S[4 * k % 16]
        for q in (1, 2, 3):
            odd = q % 2 == 1
            u[q] = u[q] + (rm if odd else rp) * C[q * k % 16]
            v[q] = v[q] + (ip if odd else im) * S[q * k % 16]
    out[0] = out[0] + u[0]
    out[4] = out[4] - v[4]
    for q in (1, 2, 3):
        out[q] = out[q] + u[q] - v[q]
        out[8 - q] = out[8 - q] - u[q] - v[q]
    return out


TILE = 16


def split(value):
    high = value.astype(BF16)
    return high, (value - high.astype(F32)).astype(BF16)


def forward_q(x_ref, a_ref, lane_ref, part):
    def step(i, _):
        rows = pl.ds(pl.multiple_of(i * TILE, TILE), TILE)
        y = dft16_half([x_ref[q, rows, :].astype(F32) for q in range(8)])
        for k in range(9):
            re, im = y[k]
            lc, ls = lane_ref[k, 0:1, :], lane_ref[k, 1:2, :]
            if k == 0:
                im = jnp.zeros_like(re)
            elif im is None:
                re, im = re * lc, -(re * ls)
            else:
                re, im = re * lc + im * ls, im * lc - re * ls
            for part, at in ((re, 0), (im, 128)):
                high, low = split(part)
                a_ref[k, rows, at : at + 128] = high
                a_ref[k, rows, at + 256 : at + 384] = low
        return 0

    lax.fori_loop(part * (256 // TILE), (part + 1) * (256 // TILE), step, 0)


def inverse_q(z_ref, emit, edge, scale, part):
    def step(i, _):
        row = pl.multiple_of(i * TILE, TILE)
        z = []
        for k in range(9):
            re = z_ref[pl.ds(1024 * k + row, TILE), :]
            im = z_ref[pl.ds(1024 * k + 512 + row, TILE), :]
            if k in (0, 8) and edge != 1.0:
                re = re * edge
            z.append((re, im))
        for q, value in enumerate(idft16_half(z)):
            emit(pl.ds(row, TILE), q, value * scale)
        return 0

    lax.fori_loop(part * (256 // TILE), (part + 1) * (256 // TILE), step, 0)


def long_dot(hi_ref, lo_ref, g_ref):
    out = jnp.dot(hi_ref[...], g_ref[...], preferred_element_type=F32)
    out = out + jnp.dot(lo_ref[...], g_ref[0:256, :], preferred_element_type=F32)
    return out[0:256], out[256:512]


def forward_k(a_ref, k, tabs, g_ref):
    hi_ref, lo_ref, tw_ref, lane_ref, cross_ref = tabs
    d = jnp.dot(a_ref[k], cross_ref[0], preferred_element_type=F32)
    r0, i0 = d[0:256, 0:128], d[0:256, 128:256]
    r1, i1 = d[256:512, 0:128], d[256:512, 128:256]
    c, s = lane_ref[k, 2:3, :], lane_ref[k, 3:4, :]
    r1, i1 = r1 * c + i1 * s, i1 * c - r1 * s
    out = []
    for kh, (re, im) in enumerate(((r0 + r1, i0 + i1), (r0 - r1, i0 - i1))):
        c, s = tw_ref[k, 256 * kh : 256 * kh + 256, 0:128], tw_ref[k, 256 * kh : 256 * kh + 256, 128:256]
        re, im = re * c + im * s, im * c - re * s
        put(g_ref.at[kh], slice(0, 256), slice(256, 512), re, im)
        c, s = long_dot(hi_ref, lo_ref, g_ref.at[kh])
        out.append((c[:, 0:128] + s[:, 128:256], c[:, 128:256] - s[:, 0:128]))
    return out


def put(ref, rows, low_rows, re, im):
    for part, at in ((re, 0), (im, 128)):
        high, low = split(part)
        ref[rows, at : at + 128] = high
        ref[low_rows, at : at + 128] = low


def inverse_k(g_ref, k, tabs, a_ref, z_ref):
    hi_ref, lo_ref, tw_ref, lane_ref, cross_ref = tabs
    b = []
    for kh in range(2):
        c, s = long_dot(hi_ref, lo_ref, g_ref.at[kh])
        re, im = c[:, 0:128] - s[:, 128:256], c[:, 128:256] + s[:, 0:128]
        c, s = tw_ref[k, 256 * kh : 256 * kh + 256, 0:128], tw_ref[k, 256 * kh : 256 * kh + 256, 128:256]
        b.append((re * c - im * s, im * c + re * s))
    (r0, i0), (r1, i1) = b
    c, s = lane_ref[k, 2:3, :], lane_ref[k, 3:4, :]
    r1, i1, r0, i0 = r0 - r1, i0 - i1, r0 + r1, i0 + i1
    r1, i1 = r1 * c - i1 * s, i1 * c + r1 * s
    for at, (re, im) in ((0, (r0, i0)), (256, (r1, i1))):
        for part, lanes in ((re, 0), (im, 128)):
            high, low = split(part)
            a_ref[at : at + 256, lanes : lanes + 128] = high
            a_ref[at : at + 256, lanes + 256 : lanes + 384] = low
    d = jnp.dot(a_ref[...], cross_ref[1], preferred_element_type=F32)
    re, im = d[:, 0:128], d[:, 128:256]
    c, s = lane_ref[k, 0:1, :], lane_ref[k, 1:2, :]
    z_ref[pl.ds(1024 * k, 512), :] = re * c - im * s
    z_ref[pl.ds(1024 * k + 512, 512), :] = im * c + re * s


def exchange_groups(blocks, swap_ref):
    return jnp.dot(jnp.concatenate(blocks, 1), swap_ref[...], preferred_element_type=F32)


def unpack_kernel(conv_ref, corr_ref, grad_ref, gate_ref, pre_ref, skip_ref, swap_ref, in_ref, gg_ref, fg_ref):
    for half in range(2):
        lanes = slice(128 * half, 128 * half + 128)
        conv = exchange_groups([conv_ref[4 * half + e] for e in range(4)], swap_ref)
        corr = exchange_groups([corr_ref[4 * half + e] for e in range(4)], swap_ref)
        skip = skip_ref[:, lanes]
        for r in range(4):
            g = grad_ref[r, :, lanes].astype(F32)
            in_ref[r, :, lanes] = conv[:, 128 * r : 128 * r + 128] + skip * (g * gate_ref[r, :, lanes].astype(F32))
            gg_ref[r, :, lanes] = (g * pre_ref[r, :, lanes].astype(F32)).astype(BF16)
            fg_ref[r, :, lanes] = corr[:, 128 * r : 128 * r + 128]


MESH = pl.DeviceIdType.MESH
OFFSETS = ((2, 0), (0, 1), (2, 1), (1, 1), (3, 0), (3, 1), (1, 0))
CHUNKS = ((0, 4), (4, 4), (8, 4), (12, 2), (14, 2))
SPEC = 9 * 1024
PACK = 256
CORR_AFTER = 3


def pack_dy(grad_ref, gate_ref, swap_ref, out_ref, part):
    for half in range(2):
        lanes = slice(128 * half, 128 * half + 128)
        at = [slice(512 * r + PACK * part, 512 * r + PACK * part + PACK) for r in range(4)]
        dy = [(grad_ref[a, lanes].astype(F32) * gate_ref[a, lanes].astype(F32)).astype(BF16) for a in at]
        dy = exchange_groups(dy, swap_ref).astype(BF16)
        for e in range(4):
            out_ref[4 * half + e, PACK * part : PACK * part + PACK, :] = dy[:, 128 * e : 128 * e + 128]


def pack_values(val_ref, swap_ref, out_ref, part):
    for half in range(2):
        lanes = slice(128 * half, 128 * half + 128)
        at = [slice(512 * r + PACK * part, 512 * r + PACK * part + PACK) for r in range(4)]
        va = exchange_groups([val_ref[a, lanes] for a in at], swap_ref).astype(BF16)
        for e in range(4):
            out_ref[4 * half + e, PACK * part : PACK * part + PACK, :] = va[:, 128 * e : 128 * e + 128]


def pack_rows(h_ref, swap_ref, rev_ref, out_ref, kq, slot, mirrored):
    parts = []
    for ri in range(2):
        for half in range(2):
            base = (2 * ri + half) * 4096 + kq
            blocks = []
            for kr in (3, 2, 1, 0) if mirrored else range(4):
                rows = [h_ref[pl.ds(base + 16 * kr + 64 * kh, 32, stride=128), :] for kh in range(2)]
                blocks.append(jnp.concatenate(rows, 0).astype(BF16))
            parts.append(jnp.concatenate(blocks, 1))
    wide = jnp.dot(jnp.concatenate(parts, 0), swap_ref[...], preferred_element_type=F32).astype(BF16)
    for n in range(4):
        rows = wide[64 * n : 64 * n + 64]
        if mirrored:
            rows = jnp.dot(rev_ref[...], rows, preferred_element_type=F32).astype(BF16)
        for e in range(4):
            out_ref[4 * (n % 2) + e, slot, n // 2] = rows[:, 128 * e : 128 * e + 128]


def pack_spectrum(h_ref, swap_ref, rev_ref, out_ref, chunk):
    first, count = CHUNKS[chunk]
    if first == 0:
        pack_rows(h_ref, swap_ref, rev_ref, out_ref, 0, 0, False)
        pack_rows(h_ref, swap_ref, rev_ref, out_ref, 8, 1, False)
        first, count = 2, count - 2

    def step(i, _):
        slot = first + 2 * i
        k = slot // 2
        pack_rows(h_ref, swap_ref, rev_ref, out_ref, k, slot, False)
        pack_rows(h_ref, swap_ref, rev_ref, out_ref, 16 - k, slot + 1, True)
        return 0

    lax.fori_loop(0, count // 2, step, 0)


def conv_block(big_ref, h_ref, tabs, g_ref, a_ref, k, slot, mirror):
    for kh in range(2):
        for p in range(8):
            at = slice(32 * kh, 32 * kh + 32)
            hr = h_ref[p, slot, 0, at, :].astype(F32)
            hi = h_ref[p, slot, 1, at, :].astype(F32)
            if mirror is not None:
                hr = hr + h_ref[7 - p, mirror, 0, at, :].astype(F32)
                hi = hi - h_ref[7 - p, mirror, 1, at, :].astype(F32)
            first = SPEC + 1024 * k + 256 * kh + 32 * p
            dr, di = big_ref[pl.ds(first, 32), :], big_ref[pl.ds(first + 512, 32), :]
            rows, low = slice(32 * p, 32 * p + 32), slice(256 + 32 * p, 288 + 32 * p)
            put(g_ref.at[kh], rows, low, hr * dr + hi * di, hr * di - hi * dr)
    inverse_k(g_ref, k, tabs, a_ref, big_ref)


def main_kernel(
    grad_hbm, gate_hbm, val_hbm, h_hbm, hi_hbm, lo_hbm, tw_hbm, cross_hbm, swap_hbm, lane_hbm, rev_hbm,
    corr_out, conv_out,
    grad_v, gate_v, val_v, hi_v, lo_v, tw_v, cross_v, swap_v, lane_v, rev_v, tok_send, tok_recv, h_send, h_recv,
    big, dy_a, val_a, inv_a, dy_g, val_g, inv_g, res_send, load_sems, own_sems, send_sems, recv_sems,
):
    me = lax.axis_index("ctx")
    x, z = me // 2, me % 2
    peers = [((x + dx) % 4) * 2 + (z + dz) % 2 for dx, dz in OFFSETS]

    barrier = pltpu.get_barrier_semaphore()
    for peer in peers:
        pl.semaphore_signal(barrier, inc=1, device_id={"ctx": peer}, device_id_type=MESH)
    loads = [(grad_hbm, grad_v), (gate_hbm, gate_v), (swap_hbm, swap_v), (val_hbm, val_v)]
    for ri in range(2):
        for half in range(2):
            loads.append((h_hbm.at[ri, :, pl.ds(128 * half, 128)], big.at[pl.ds((2 * ri + half) * 4096, 4096), :]))
    loads += [(rev_hbm, rev_v), (lane_hbm, lane_v), (tw_hbm, tw_v), (hi_hbm, hi_v), (lo_hbm, lo_v), (cross_hbm, cross_v)]
    loads = [pltpu.make_async_copy(a, b, load_sems.at[i]) for i, (a, b) in enumerate(loads)]
    for c in loads[:4]:
        c.start()

    def exchange(group, source, target):
        copies = []
        for i, peer in enumerate(peers):
            c = pltpu.make_async_remote_copy(
                src_ref=source(peer), dst_ref=target,
                send_sem=send_sems.at[group, i], recv_sem=recv_sems.at[group, i],
                device_id={"ctx": peer}, device_id_type=MESH,
            )
            c.start()
            copies.append(c)
        own = pltpu.make_async_copy(source(me), target, own_sems.at[group])
        own.start()
        return copies, own

    def arrived(pair):
        for c in pair[0]:
            c.wait_recv()
        pair[1].wait()

    halves = [pl.ds(256 * part, 256) for part in range(2)]
    for c in loads[:3]:
        c.wait()
    dy_moves, val_moves, h_moves = [], [], []
    for part, at in enumerate(halves):
        pack_dy(grad_v, gate_v, swap_v, tok_send.at[0], part)
        if part == 0:
            pl.semaphore_wait(barrier, 7)
        dy_moves.append(exchange(part, lambda d: tok_send.at[0, d, at], tok_recv.at[0, me, at]))
    for c in loads[4:]:
        c.start()
    loads[3].wait()
    for part, at in enumerate(halves):
        pack_values(val_v, swap_v, tok_send.at[1], part)
        val_moves.append(exchange(2 + part, lambda d: tok_send.at[1, d, at], tok_recv.at[1, me, at]))
    for c in loads[4:9]:
        c.wait()
    for chunk, (first, count) in enumerate(CHUNKS):
        pack_spectrum(big, swap_v, rev_v, h_send, chunk)
        at = pl.ds(first, count)
        h_moves.append(exchange(4 + chunk, lambda d: h_send.at[d, at], h_recv.at[me, at]))
    for c in loads[9:]:
        c.wait()

    tabs = (hi_v, lo_v, tw_v, lane_v, cross_v)
    for n, (moves, a_ref) in enumerate(((dy_moves, dy_a), (val_moves, val_a))):
        for part in range(2):
            arrived(moves[part])
            forward_q(tok_recv.at[n], a_ref, lane_v, part)

    def block(k, _):
        dy_s = forward_k(dy_a, k, tabs, dy_g)
        val_s = forward_k(val_a, k, tabs, val_g)
        for kh in range(2):
            (dr, di), (vr, vi) = dy_s[kh], val_s[kh]
            first = SPEC + 1024 * k + 256 * kh
            big[pl.ds(first, 256), :] = dr
            big[pl.ds(first + 512, 256), :] = di
            put(inv_g.at[kh], slice(0, 256), slice(256, 512), vr * dr + vi * di, vr * di - vi * dr)
        inverse_k(inv_g, k, tabs, inv_a, big)
        return 0

    lax.fori_loop(0, 9, block, 0)

    def emit_to(n):
        def emit(rows, q, value):
            res_send[n, q, rows, :] = value.astype(BF16)
        return emit

    for part in range(2):
        inverse_q(big, emit_to(0), 0.5, 2.0 / N, part)

    conv_moves = []
    for chunk, (first, count) in enumerate(CHUNKS):
        arrived(h_moves[chunk])
        if chunk == CORR_AFTER:
            corr_move = exchange(9, lambda d: res_send.at[0, d], corr_out.at[me])
        if first == 0:
            conv_block(big, h_recv, tabs, inv_g, inv_a, 0, 0, None)
            conv_block(big, h_recv, tabs, inv_g, inv_a, 8, 1, None)
            first, count = 2, count - 2

        def step(i, _, first=first):
            slot = first + 2 * i
            conv_block(big, h_recv, tabs, inv_g, inv_a, slot // 2, slot, slot + 1)
            return 0

        lax.fori_loop(0, count // 2, step, 0)
    for part in range(2):
        inverse_q(big, emit_to(1), 1.0, 1.0 / N, part)
        at = halves[part]
        conv_moves.append(exchange(10 + part, lambda d: res_send.at[1, d, at], conv_out.at[me, at]))
    moves = (*dy_moves, *val_moves, *h_moves, corr_move, *conv_moves)
    for pair in (corr_move, *conv_moves):
        arrived(pair)
    for pair in moves:
        for c in pair[0]:
            c.wait_send()


def on_device(grad_out, values, gate, pre_gate, filter_spectrum, skip):
    S_ = jax.ShapeDtypeStruct
    hi, lo, tw, lane, cross, swap, rev = (jnp.asarray(a) for a in tables())
    anywhere = pl.BlockSpec(memory_space=pl.ANY)
    result = pltpu.VMEM((8, 512, 128), BF16)
    tokens = pltpu.VMEM((2048, 256), BF16)
    corr, conv = pl.pallas_call(
        main_kernel,
        out_shape=(result, result),
        in_specs=[anywhere] * 11,
        out_specs=(anywhere, anywhere),
        scratch_shapes=[
            tokens,
            tokens,
            tokens,
            pltpu.VMEM((512, 512), BF16),
            pltpu.VMEM((512, 256), BF16),
            pltpu.VMEM((9, 512, 256), F32),
            pltpu.VMEM((2, 512, 256), BF16),
            pltpu.VMEM((512, 512), BF16),
            pltpu.VMEM((9, 8, 128), F32),
            pltpu.VMEM((64, 64), BF16),
            pltpu.VMEM((2, 8, 512, 128), BF16),
            pltpu.VMEM((2, 8, 512, 128), BF16),
            pltpu.VMEM((8, 16, 2, 64, 128), BF16),
            pltpu.VMEM((8, 16, 2, 64, 128), BF16),
            pltpu.VMEM((18 * 1024, 128), F32),
            pltpu.VMEM((9, 512, 512), BF16),
            pltpu.VMEM((9, 512, 512), BF16),
            pltpu.VMEM((512, 512), BF16),
            pltpu.VMEM((2, 512, 256), BF16),
            pltpu.VMEM((2, 512, 256), BF16),
            pltpu.VMEM((2, 512, 256), BF16),
            pltpu.VMEM((2, 8, 512, 128), BF16),
            pltpu.SemaphoreType.DMA((14,)),
            pltpu.SemaphoreType.DMA((12,)),
            pltpu.SemaphoreType.DMA((12, 7)),
            pltpu.SemaphoreType.DMA((12, 7)),
        ],
        compiler_params=pltpu.CompilerParams(collective_id=0, has_side_effects=True, vmem_limit_bytes=58 << 20),
    )(grad_out, gate, values, filter_spectrum, hi, lo, tw, cross, swap, lane, rev)

    rows = 256
    packed = pl.BlockSpec((8, rows, 128), lambda i: (0, i, 0))
    plain = pl.BlockSpec((4, rows, 256), lambda i: (0, i, 0))
    whole = lambda shape: pl.BlockSpec(shape, lambda i: (0, 0))
    fold = lambda a: a.reshape(4, 512, 256)
    outs = pl.pallas_call(
        unpack_kernel,
        grid=(512 // rows,),
        out_shape=(S_((4, 512, 256), F32), S_((4, 512, 256), BF16), S_((4, 512, 256), F32)),
        in_specs=[packed, packed, plain, plain, plain, whole((1, 256)), whole((512, 512))],
        out_specs=(plain, plain, plain),
        compiler_params=pltpu.CompilerParams(vmem_limit_bytes=32 << 20),
    )(conv, corr, fold(grad_out), fold(gate), fold(pre_gate), skip.reshape(1, 256), swap)
    return tuple(a.reshape(2048, 256) for a in outs)


def solution(mesh):
    rows = P("ctx", "chan")
    return jax.shard_map(
        on_device,
        mesh=mesh,
        in_specs=(rows, rows, rows, rows, P(None, "ctx", "chan"), P("chan")),
        out_specs=(rows, rows, rows),
        check_vma=False,
    )
```
